512 devices in a mesh: panel: 2 (over core), lon: 32 (over x, y), lat: 8 (over z).
Axes of the slice: x: 4, y: 8, z: 8, core: 2. Of those that a mesh axis runs over, the one named last changes fastest.
Arguments:
- fields: float32 [2, 24, 1024, 1024], P('panel', None, 'lon', 'lat'), may hold values from -6 to 6
- offsets: int32 [2, 2, 128, 8], P('panel', None, 'lon', 'lat'), may hold values from -7 to 7
- fractions: float32 [2, 2, 1024, 1024], P('panel', None, 'lon', 'lat'), may hold values from 0 to 1
- send_count: int32 [2, 32, 8], P('panel', 'lon', 'lat'), may hold values from 0 to 16, as said below
- send_owner: int32 [2, 32, 8, 16], P('panel', 'lon', 'lat'), may hold values from 0 to 31, as said below
- send_cell: int32 [2, 32, 8, 16], P('panel', 'lon', 'lat'), may hold values from 0 to 3966, as said below
- send_target: int32 [2, 32, 8, 16], P('panel', 'lon', 'lat'), may hold values from 0 to 127, as said below
- send_frac: float32 [2, 32, 8, 2, 16], P('panel', 'lon', 'lat'), may hold values from 0 to 1
Outputs:
- advected_fields: float32 [2, 24, 1024, 1024], P('panel', None, 'lon', 'lat')
The draws below stay inside these ranges and needn't reach their ends.
Inputs may be any that keep to these rules, and one draw needn't show every extreme that they name: `send_count`: 16 on the devices that give donor values and 0 elsewhere; in each row of devices along longitude (one panel, one latitude index) the donors are the first 16 or the last 16 longitude indices. `send_owner`: the receiving device lies on the other panel at the same latitude index and is at the first or the last longitude index; the live slots of a donor name each of the two exactly 8 times. `send_cell`: lon_row * 128 + lat_col with lon_row < 31 and lat_col < 127. `send_target`: over the live slots of all donors that fill one receiving device, every value from 0 to 127 appears exactly once.
All inputs are finite; a program needn't handle non-finite values.
Results may differ from the reference program's by a relative error of at most 0.00002.
Values sent between devices are 32-bit elements; how exact they have to be, the bound alone decides.
No kernel may reach another device: no remote copies, remote signals or barrier semaphores. Data moves between devices by JAX's collectives and lax.ppermute only.
A program may use at most 64 MiB of HBM per device.

```python
import jax
import jax.numpy as jnp
from jax import lax

FIELDS = 6
LEVELS = 4
CLON = 32
CLAT = 128
TILE = 8
BLOCK = 128
REACH = 7
HALO = 9
NLON = 1024
NLAT = 1024
BAND = 16
CAP = 8
SLOTS = 16
N_LON = 32
N_LAT = 8


def border_plan(key):
    lon_count = NLON // CLON
    lat_count = NLAT // CLAT
    band_key, perm_key, shuffle_key = jax.random.split(key, 3)
    band_start = (jax.random.randint(band_key, (2, lat_count), 0, 2) * (lon_count - BAND)).astype(jnp.int32)
    perm_keys = jax.random.split(perm_key, 2 * lat_count * 2)
    rim_perms = jax.vmap(lambda k: jax.random.permutation(k, CLAT))(perm_keys).reshape(2, lat_count, 2, CLAT).astype(jnp.int32)
    shuffle_keys = jax.random.split(shuffle_key, 2 * lon_count * lat_count)
    shuffles = jax.vmap(lambda k: jax.random.permutation(k, SLOTS))(shuffle_keys).reshape(2, lon_count, lat_count, SLOTS).astype(jnp.int32)
    donor_panel = jnp.arange(2, dtype=jnp.int32)[:, None, None]
    lon_index = jnp.arange(lon_count, dtype=jnp.int32)[None, :, None]
    lat_index = jnp.arange(lat_count, dtype=jnp.int32)[None, None, :]
    recv_panel = 1 - donor_panel
    position = lon_index - band_start[recv_panel, lat_index]
    is_live = (position >= 0) & (position < BAND)
    live_count = jnp.where(is_live, SLOTS, 0).astype(jnp.int32)
    slot_index = jnp.arange(SLOTS, dtype=jnp.int32)
    rim_side = slot_index // CAP
    within = slot_index % CAP
    donor_slot = jnp.clip(position, 0, BAND - 1)[..., None] * CAP + within
    target = rim_perms[recv_panel[..., None], lat_index[..., None], rim_side, donor_slot]
    owner_lon = jnp.broadcast_to(rim_side * (lon_count - 1), target.shape).astype(jnp.int32)
    target = jnp.take_along_axis(target, shuffles, axis=-1)
    owner_lon = jnp.take_along_axis(owner_lon, shuffles, axis=-1)
    return (live_count, owner_lon, target)


def draw_send_count(key, part):
    return border_plan(key)[0]


def draw_send_owner(key, part):
    return border_plan(key)[1]


def draw_send_target(key, part):
    return border_plan(key)[2]


def draw_send_cell(key, part):
    key = jax.random.fold_in(key, 7)
    lon_count = NLON // CLON
    lat_count = NLAT // CLAT
    row_key, col_key = jax.random.split(key)
    shape = (2, lon_count, lat_count, SLOTS)
    cell_row = jax.random.randint(row_key, shape, 0, CLON - 1)
    cell_col = jax.random.randint(col_key, shape, 0, CLAT - 1)
    cell_row = cell_row.at[0, 0, 0, 0].set(0).at[0, 0, 0, 1].set(CLON - 2)
    cell_col = cell_col.at[0, 0, 0, 0].set(0).at[0, 0, 0, 1].set(CLAT - 2)
    return (cell_row * CLAT + cell_col).astype(jnp.int32)


def touch_ends(array, own_key, low, top_value):
    index_at = [jax.random.randint(jax.random.fold_in(own_key, axis), (), 0, length) for axis, length in enumerate(array.shape)]
    widest = array.shape.index(max(array.shape))
    neighbour = index_at[:widest] + [(index_at[widest] + 1) % array.shape[widest]] + index_at[widest + 1:]
    return array.at[tuple(index_at)].set(low).at[tuple(neighbour)].set(top_value)


def block_levels(rng, dims, cuts, low, largest):
    loudness, own = 1.0, jax.random.fold_in(rng, 6)
    for dim, shards_of in cuts:
        steps = jnp.exp(jax.random.uniform(jax.random.fold_in(own, dim), (shards_of,), jnp.float32, low / len(cuts), largest / len(cuts)))
        loudness = loudness * jnp.repeat(steps, dims[dim] // shards_of).reshape([-1 if axis == dim else 1 for axis in range(len(dims))])
    return loudness


def scatter_about(stream_key, shape, width, reach, shards=(), held_as=jnp.bfloat16):
    array = width * jax.random.normal(stream_key, shape, jnp.float32)
    if shards:
        array = array * block_levels(stream_key, shape, shards, -0.22, 0.18)
    return jnp.clip(array, -reach, reach).astype(held_as)


def setup_inputs(seed: int = 0) -> dict:
    seeds = jax.random.split(jax.random.key(seed), 9)
    return {
        "fields": scatter_about(seeds[0], (2, FIELDS * LEVELS, NLON, NLAT), 1.0, 6.0, ((0, 2), (2, 32), (3, 8)), jnp.float32),
        "offsets": touch_ends(jax.random.randint(seeds[1], (2, 2, NLON // TILE, NLAT // BLOCK), -REACH, REACH + 1), jax.random.fold_in(seeds[1], 1), -REACH, REACH).astype(jnp.int32),
        "fractions": jnp.clip(1.0 * jax.random.uniform(seeds[2], (2, 2, NLON, NLAT), jnp.float32) ** block_levels(seeds[2], (2, 2, NLON, NLAT), ((0, 2), (2, 32), (3, 8)), -0.2, 0.2), 0.0, 1.0),
        "send_count": draw_send_count(jax.random.fold_in(seeds[8], 71), 0),
        "send_owner": draw_send_owner(jax.random.fold_in(seeds[8], 71), 0),
        "send_cell": draw_send_cell(jax.random.fold_in(seeds[8], 71), 0),
        "send_target": draw_send_target(jax.random.fold_in(seeds[8], 71), 0),
        "send_frac": jnp.clip(1.0 * jax.random.uniform(seeds[7], (2, N_LON, N_LAT, 2, SLOTS), jnp.float32) ** block_levels(seeds[7], (2, N_LON, N_LAT, 2, SLOTS), ((0, 2), (1, 32), (2, 8)), -0.2, 0.2), 0.0, 1.0),
    }


def lagrange(x):
    return (-x * (x - 1.0) * (x - 2.0) / 6.0, (x + 1.0) * (x - 1.0) * (x - 2.0) / 2.0,
            -(x + 1.0) * x * (x - 2.0) / 2.0, (x + 1.0) * x * (x - 1.0) / 6.0)


def interpolate(window, frac_lon, frac_lat):
    lon_weights = lagrange(frac_lon)
    lat_weights = lagrange(frac_lat)
    summed = jnp.zeros((window.shape[0], TILE, BLOCK), jnp.float32)
    for a in range(4):
        inner_sum = jnp.zeros((window.shape[0], TILE, BLOCK), jnp.float32)
        for b in range(4):
            inner_sum = inner_sum + lat_weights[b] * window[:, a:a + TILE, b:b + BLOCK]
        summed = summed + lon_weights[a] * inner_sum
    return summed


def advect(padded, offsets, fractions, halo_width):
    tiles_lon = offsets.shape[1]
    tiles_lat = offsets.shape[2]
    channels = padded.shape[0]

    def one_row(t):
        def one_tile(u):
            start_lon = t * TILE + halo_width + offsets[0, t, u] - 1
            start_lat = u * BLOCK + halo_width + offsets[1, t, u] - 1
            window = lax.dynamic_slice(padded, (jnp.int32(0), start_lon, start_lat), (channels, TILE + 3, BLOCK + 3))
            frac_tile = lax.dynamic_slice(fractions, (jnp.int32(0), t * TILE, u * BLOCK), (2, TILE, BLOCK))
            return interpolate(window, frac_tile[0], frac_tile[1])
        return jax.vmap(one_tile)(jnp.arange(tiles_lat, dtype=jnp.int32))

    tiled = lax.map(one_row, jnp.arange(tiles_lon, dtype=jnp.int32))
    return tiled.transpose(2, 0, 3, 1, 4).reshape(channels, tiles_lon * TILE, tiles_lat * BLOCK)


def bilinear(base_val, lat_next, lon_next, diagonal_next, a, b):
    return (1.0 - a) * (1.0 - b) * base_val + (1.0 - a) * b * lat_next + a * (1.0 - b) * lon_next + a * b * diagonal_next


def reference(fields, offsets, fractions, send_count, send_owner, send_cell, send_target, send_frac):
    advected = jnp.stack([advect(jnp.pad(fields[p], ((0, 0), (HALO, HALO), (HALO, HALO))), offsets[p], fractions[p], HALO) for p in range(2)])
    lon_count = NLON // CLON
    lat_count = NLAT // CLAT
    slot_count = send_owner.shape[-1]
    panel_index = jnp.arange(2, dtype=jnp.int32)[:, None, None, None]
    lon_index = jnp.arange(lon_count, dtype=jnp.int32)[None, :, None, None]
    lat_index = jnp.arange(lat_count, dtype=jnp.int32)[None, None, :, None]
    src_row = lon_index * CLON + send_cell // CLAT
    src_col = lat_index * CLAT + send_cell % CLAT
    base_val = advected[panel_index, :, src_row, src_col]
    lat_next = advected[panel_index, :, src_row, src_col + 1]
    lon_next = advected[panel_index, :, src_row + 1, src_col]
    diagonal_next = advected[panel_index, :, src_row + 1, src_col + 1]
    frac_a = send_frac[:, :, :, 0, :][..., None]
    frac_b = send_frac[:, :, :, 1, :][..., None]
    donor = bilinear(base_val, lat_next, lon_next, diagonal_next, frac_a, frac_b)
    is_live = jnp.arange(slot_count, dtype=jnp.int32)[None, None, None, :] < send_count[..., None]
    dest_row = jnp.where(send_owner == 0, 0, NLON - 1).astype(jnp.int32)
    dest_col = jnp.where(is_live, lat_index * CLAT + send_target, NLAT).astype(jnp.int32)
    return advected.at[1 - panel_index, :, dest_row, dest_col].set(donor, mode="drop")
```

```python
import jax
import jax.numpy as jnp
from jax import lax
from jax.experimental import pallas as pl
from jax.experimental.pallas import tpu as pltpu
from jax.sharding import PartitionSpec as P

TILE = 8
LOW = 8
HIGH = 9
WINDOW = TILE + 3
LANES = 128
PITCH = 16
GROUP = LANES // PITCH
FIELD = 32

VMEM = pl.BlockSpec(memory_space=pltpu.VMEM)
SMEM = pl.BlockSpec(memory_space=pltpu.SMEM)
ANY = pl.BlockSpec(memory_space=pl.ANY)


def lane_iota(shape):
    return lax.broadcasted_iota(jnp.int32, shape, len(shape) - 1)


def pack_kernel(cells_ref, rows_ref, first_ref, last_ref):
    channels, lanes = rows_ref.shape[1:]
    row_count = rows_ref.shape[0]
    lane = lane_iota((channels, lanes))
    for m in range(row_count // GROUP):
        first = last = None
        for s in range(GROUP):
            i = m * GROUP + s
            row = cells_ref[pl.ds(i, channels, stride=row_count), :]
            rows_ref[i] = row
            turned = row if s == 0 else pltpu.roll(row, PITCH * s, 1)
            if s == 0:
                first = last = turned
            else:
                base = PITCH * s
                first = jnp.where((lane >= base) & (lane < base + HIGH), turned, first)
                last = jnp.where((lane >= base - LOW) & (lane < base), turned, last)
        first_ref[m] = first
        last_ref[m] = last


def weight_kernel(fractions_ref, weights_ref):
    for axis in range(2):
        x = fractions_ref[axis]
        weights_ref[4 * axis] = -x * (x - 1.0) * (x - 2.0) / 6.0
        weights_ref[4 * axis + 1] = (x + 1.0) * (x - 1.0) * (x - 2.0) / 2.0
        weights_ref[4 * axis + 2] = -(x + 1.0) * x * (x - 2.0) / 2.0
        weights_ref[4 * axis + 3] = (x + 1.0) * x * (x - 1.0) / 6.0


def edge_kernel(rows_ref, west_ref, east_ref, to_next_ref, to_prev_ref):
    row_count, channels, lanes = rows_ref.shape
    to_next_ref[0:LOW] = rows_ref[row_count - LOW : row_count]
    to_next_ref[LOW] = west_ref[row_count // GROUP - 1]
    to_next_ref[LOW + 1] = east_ref[row_count // GROUP - 1]
    to_prev_ref[0:HIGH] = rows_ref[0:HIGH]
    to_prev_ref[HIGH] = west_ref[0]
    to_prev_ref[HIGH + 1] = east_ref[0]
    lane = lane_iota((channels, lanes))
    to_prev_ref[HIGH + 2] = jnp.where(lane < lanes // 2, east_ref[1], west_ref[1])


def advect_kernel(
    offsets_ref, count_ref, owner_ref, cell_ref, target_ref, frac_ref,
    rows_ref, west_ref, east_ref, prev_ref, next_ref, weights_ref,
    advected_ref, message_ref,
    ext_ref, west_ext_ref, east_ext_ref, shifted_ref,
):
    row_count, channels, lanes = rows_ref.shape
    groups = row_count // GROUP
    ext_ref[0:LOW] = prev_ref[0:LOW]
    ext_ref[LOW : LOW + row_count] = rows_ref[...]
    ext_ref[LOW + row_count : LOW + row_count + HIGH] = next_ref[0:HIGH]
    west_ext_ref[0] = prev_ref[LOW]
    east_ext_ref[0] = prev_ref[LOW + 1]
    west_ext_ref[1 : 1 + groups] = west_ref[...]
    east_ext_ref[1 : 1 + groups] = east_ref[...]
    west_ext_ref[1 + groups] = next_ref[HIGH]
    east_ext_ref[1 + groups] = next_ref[HIGH + 1]
    west_ext_ref[2 + groups] = next_ref[HIGH + 2]
    east_ext_ref[2 + groups] = next_ref[HIGH + 2]

    lane = lane_iota((channels, lanes))
    within = lane & (PITCH - 1)
    for t in range(row_count // TILE):
        offset_lon = offsets_ref[0, 0, t]
        offset_lat = offsets_ref[1, 0, t]
        start = t * TILE + LOW - 1 + offset_lon
        from_east = within < LOW + jnp.where(offset_lat == HIGH - 2, 1, 0)
        for j in range(WINDOW):
            e = start + j
            center = ext_ref[e]
            packed = jnp.where(from_east, east_ext_ref[e >> 3], west_ext_ref[e >> 3])
            halo = pltpu.roll(packed, (LANES - PITCH * (e & 7)) & (LANES - 1), 1)
            for b in range(4):
                shift = offset_lat - 1 + b
                inside = (lane >= shift) & (lane < LANES + shift)
                shifted_ref[t, b, j] = pltpu.roll(
                    jnp.where(inside, center, halo), (LANES - shift) & (LANES - 1), 1
                )
        for i in range(TILE):
            row = t * TILE + i
            lat_weights = [weights_ref[4 + b, row : row + 1, :] for b in range(4)]
            total = None
            for a in range(4):
                inner = lat_weights[0] * shifted_ref[t, 0, i + a]
                for b in range(1, 4):
                    inner = inner + lat_weights[b] * shifted_ref[t, b, i + a]
                part = weights_ref[a, row : row + 1, :] * inner
                total = part if total is None else total + part
            advected_ref[row] = total

    channel = lax.broadcasted_iota(jnp.int32, (channels, lanes), 0)
    one_lane = lane_iota((1, lanes))
    slots = owner_ref.shape[1]
    capacity = slots // 2
    halves = capacity * FIELD // lanes
    per_row = lanes // FIELD
    sums = [jnp.zeros((channels, lanes), jnp.float32) for _ in range(2 * halves)]
    empty = jnp.where((one_lane & (FIELD - 1)) == channels, jnp.float32(lanes), jnp.float32(0.0))
    places = [empty for _ in range(2 * halves)]
    taken = [jnp.int32(0), jnp.int32(0)]
    for k in range(slots):
        cell = cell_ref[0, k]
        r, c = cell >> 7, cell & (lanes - 1)
        a, b = frac_ref[0, k], frac_ref[1, k]
        near = jnp.where(one_lane == c, 1.0 - b, jnp.where(one_lane == c + 1, b, 0.0))
        value = jnp.sum(
            advected_ref[r] * ((1.0 - a) * near) + advected_ref[r + 1] * (a * near),
            axis=1,
            keepdims=True,
        )
        live = k < count_ref[0, 0]
        side = (owner_ref[0, k] != 0).astype(jnp.int32)
        target = target_ref[0, k].astype(jnp.float32)
        position = jnp.where(side == 0, taken[0], taken[1])
        taken[0] = taken[0] + jnp.where(live & (side == 0), 1, 0)
        taken[1] = taken[1] + jnp.where(live & (side == 1), 1, 0)
        base = (position % per_row) * FIELD
        here = jnp.where(live, side * halves + position // per_row, -1)
        at_value = lane - channel
        for h in range(2 * halves):
            lane_base = jnp.where(here == h, base, -lanes)
            sums[h] = jnp.where(at_value == lane_base, value, sums[h])
            places[h] = jnp.where(one_lane == lane_base + channels, target, places[h])
    lon_count = message_ref.shape[0] // 2
    other = (1 - lax.axis_index("panel")) * lon_count
    message_ref[...] = jnp.zeros_like(message_ref)
    for side in range(2):
        parts = []
        for h in range(halves):
            n = side * halves + h
            parts.append(jnp.sum(sums[n], axis=0, keepdims=True) + places[n])
        message_ref[other + side * (lon_count - 1)] = jnp.concatenate(parts, axis=1)


def column_kernel(advected_ref, out_ref):
    row_count, channels, _ = advected_ref.shape
    for i in range(row_count):
        out_ref[pl.ds(i, channels, stride=row_count), :] = advected_ref[i]


def rim_kernel(received_ref, given_ref, out_ref, rim_ref, sem):
    del given_ref
    channels, row_count, lanes = out_ref.shape
    lon = lax.axis_index("lon")
    lon_count = lax.axis_size("lon")

    @pl.when((lon == 0) | (lon == lon_count - 1))
    def _():
        other = (1 - lax.axis_index("panel")) * lon_count
        values = received_ref[pl.ds(other, lon_count)].reshape(lon_count, received_ref.shape[2])
        lane = lane_iota((lon_count, lanes))
        rim = jnp.zeros((FIELD, lanes), jnp.float32)
        for q in range(received_ref.shape[2] // FIELD):
            entry = values[:, q * FIELD : (q + 1) * FIELD]
            place = entry[:, channels : channels + 1].astype(jnp.int32)
            rim = rim + lax.dot_general(
                entry,
                jnp.where(lane == place, 1.0, 0.0),
                (((0,), (0,)), ((), ())),
                precision=lax.Precision.HIGHEST,
                preferred_element_type=jnp.float32,
            )
        rim_ref[...] = rim[0:channels].reshape(channels, 1, lanes)

        @pl.when(lon == 0)
        def _():
            copy = pltpu.make_async_copy(rim_ref, out_ref.at[:, pl.ds(0, 1), :], sem)
            copy.start()
            copy.wait()

        @pl.when(lon == lon_count - 1)
        def _():
            copy = pltpu.make_async_copy(rim_ref, out_ref.at[:, pl.ds(row_count - 1, 1), :], sem)
            copy.start()
            copy.wait()


def f32(*shape):
    return jax.ShapeDtypeStruct(shape, jnp.float32)


def up(array, axis):
    count = lax.axis_size(axis)
    return lax.ppermute(array, axis, [(i, i + 1) for i in range(count - 1)])


def down(array, axis):
    count = lax.axis_size(axis)
    return lax.ppermute(array, axis, [(i + 1, i) for i in range(count - 1)])


def body(fields, offsets, fractions, send_count, send_owner, send_cell, send_target, send_frac):
    _, channels, row_count, lanes = fields.shape
    groups = row_count // GROUP
    lon_count = lax.axis_size("lon")
    slots = send_owner.shape[-1]
    width = slots // 2 * FIELD
    ext = LOW + row_count + HIGH

    rows, first, last = pl.pallas_call(
        pack_kernel,
        out_shape=(
            f32(row_count, channels, lanes),
            f32(groups, channels, lanes),
            f32(groups, channels, lanes),
        ),
        in_specs=[VMEM],
        out_specs=(VMEM, VMEM, VMEM),
        name="pack",
    )(fields.reshape(channels * row_count, lanes))
    west = up(last, "lat")
    east = down(first, "lat")
    weights = pl.pallas_call(
        weight_kernel,
        out_shape=f32(8, row_count, lanes),
        in_specs=[VMEM],
        out_specs=VMEM,
        cost_estimate=pl.CostEstimate(flops=200000, bytes_accessed=200000, transcendentals=0),
        name="weights",
    )(fractions[0])
    to_next, to_prev = pl.pallas_call(
        edge_kernel,
        out_shape=(f32(LOW + 2, channels, lanes), f32(HIGH + 3, channels, lanes)),
        in_specs=[VMEM] * 3,
        out_specs=(VMEM, VMEM),
        name="edges",
    )(rows, west, east)
    from_prev = up(to_next, "lon")
    from_next = down(to_prev, "lon")
    advected, message = pl.pallas_call(
        advect_kernel,
        out_shape=(f32(row_count, channels, lanes), f32(2 * lon_count, 1, width)),
        in_specs=[SMEM] * 6 + [VMEM] * 6,
        out_specs=(VMEM, VMEM),
        scratch_shapes=[
            pltpu.VMEM((ext, channels, lanes), jnp.float32),
            pltpu.VMEM((groups + 3, channels, lanes), jnp.float32),
            pltpu.VMEM((groups + 3, channels, lanes), jnp.float32),
            pltpu.VMEM((row_count // TILE, 4, WINDOW, channels, lanes), jnp.float32),
        ],
        compiler_params=pltpu.CompilerParams(vmem_limit_bytes=24 * 1024 * 1024),
        name="advect",
    )(
        offsets[0].transpose(0, 2, 1),
        send_count[0],
        send_owner[0, 0],
        send_cell[0, 0],
        send_target[0, 0],
        send_frac[0, 0, 0],
        rows,
        west,
        east,
        from_prev,
        from_next,
        weights,
    )
    received = lax.all_to_all(message, ("panel", "lon"), split_axis=0, concat_axis=0, tiled=True)
    columns = pl.pallas_call(
        column_kernel,
        out_shape=f32(channels * row_count, lanes),
        in_specs=[VMEM],
        out_specs=VMEM,
        cost_estimate=pl.CostEstimate(flops=0, bytes_accessed=2000000, transcendentals=0),
        name="columns",
    )(advected)
    out = pl.pallas_call(
        rim_kernel,
        out_shape=f32(channels, row_count, lanes),
        in_specs=[VMEM, ANY],
        out_specs=ANY,
        scratch_shapes=[
            pltpu.VMEM((channels, 1, lanes), jnp.float32),
            pltpu.SemaphoreType.DMA(()),
        ],
        input_output_aliases={1: 0},
        name="rim",
    )(received, columns.reshape(channels, row_count, lanes))
    return out[None]


def solution(mesh):
    placed = (
        P("panel", None, "lon", "lat"),
        P("panel", None, "lon", "lat"),
        P("panel", None, "lon", "lat"),
        P("panel", "lon", "lat"),
        P("panel", "lon", "lat", None),
        P("panel", "lon", "lat", None),
        P("panel", "lon", "lat", None),
        P("panel", "lon", "lat", None, None),
    )
    return jax.shard_map(
        body, mesh=mesh, in_specs=placed, out_specs=P("panel", None, "lon", "lat"), check_vma=False
    )
```

```python
import jax
import jax.numpy as jnp
from jax import lax
from jax.experimental import pallas as pl
from jax.experimental.pallas import tpu as pltpu
from jax.sharding import PartitionSpec as P

TILE = 8
LOW = 8
HIGH = 9
WINDOW = TILE + 3
LANES = 128
PITCH = 16
GROUP = LANES // PITCH
FIELD = 32

VMEM = pl.BlockSpec(memory_space=pltpu.VMEM)
SMEM = pl.BlockSpec(memory_space=pltpu.SMEM)
ANY = pl.BlockSpec(memory_space=pl.ANY)


def lane_iota(shape):
    return lax.broadcasted_iota(jnp.int32, shape, len(shape) - 1)


def pack_kernel(cells_ref, rows_ref, first_ref, last_ref):
    channels, lanes = rows_ref.shape[1:]
    row_count = rows_ref.shape[0]
    lane = lane_iota((channels, lanes))
    for m in range(row_count // GROUP):
        first = last = None
        for s in range(GROUP):
            i = m * GROUP + s
            row = cells_ref[pl.ds(i, channels, stride=row_count), :]
            rows_ref[i] = row
            turned = row if s == 0 else pltpu.roll(row, PITCH * s, 1)
            if s == 0:
                first = last = turned
            else:
                base = PITCH * s
                first = jnp.where((lane >= base) & (lane < base + HIGH), turned, first)
                last = jnp.where((lane >= base - LOW) & (lane < base), turned, last)
        first_ref[m] = first
        last_ref[m] = last


def weight_kernel(fractions_ref, weights_ref):
    for axis in range(2):
        x = fractions_ref[axis]
        weights_ref[4 * axis] = -x * (x - 1.0) * (x - 2.0) / 6.0
        weights_ref[4 * axis + 1] = (x + 1.0) * (x - 1.0) * (x - 2.0) / 2.0
        weights_ref[4 * axis + 2] = -(x + 1.0) * x * (x - 2.0) / 2.0
        weights_ref[4 * axis + 3] = (x + 1.0) * x * (x - 1.0) / 6.0


def edge_kernel(rows_ref, west_ref, east_ref, to_next_ref, to_prev_ref):
    row_count, channels, lanes = rows_ref.shape
    to_next_ref[0:LOW] = rows_ref[row_count - LOW : row_count]
    to_next_ref[LOW] = west_ref[row_count // GROUP - 1]
    to_next_ref[LOW + 1] = east_ref[row_count // GROUP - 1]
    to_prev_ref[0:HIGH] = rows_ref[0:HIGH]
    to_prev_ref[HIGH] = west_ref[0]
    to_prev_ref[HIGH + 1] = east_ref[0]
    lane = lane_iota((channels, lanes))
    to_prev_ref[HIGH + 2] = jnp.where(lane < lanes // 2, east_ref[1], west_ref[1])


def advect_kernel(
    offsets_ref, count_ref, owner_ref, cell_ref, target_ref, frac_ref,
    rows_ref, west_ref, east_ref, prev_ref, next_ref, weights_ref,
    advected_ref, message_ref,
    ext_ref, west_ext_ref, east_ext_ref, shifted_ref,
):
    row_count, channels, lanes = rows_ref.shape
    groups = row_count // GROUP
    ext_ref[0:LOW] = prev_ref[0:LOW]
    ext_ref[LOW : LOW + row_count] = rows_ref[...]
    ext_ref[LOW + row_count : LOW + row_count + HIGH] = next_ref[0:HIGH]
    west_ext_ref[0] = prev_ref[LOW]
    east_ext_ref[0] = prev_ref[LOW + 1]
    west_ext_ref[1 : 1 + groups] = west_ref[...]
    east_ext_ref[1 : 1 + groups] = east_ref[...]
    west_ext_ref[1 + groups] = next_ref[HIGH]
    east_ext_ref[1 + groups] = next_ref[HIGH + 1]
    west_ext_ref[2 + groups] = next_ref[HIGH + 2]
    east_ext_ref[2 + groups] = next_ref[HIGH + 2]

    lane = lane_iota((channels, lanes))
    within = lane & (PITCH - 1)
    for t in range(row_count // TILE):
        offset_lon = offsets_ref[0, 0, t]
        offset_lat = offsets_ref[1, 0, t]
        start = t * TILE + LOW - 1 + offset_lon
        from_east = within < LOW + jnp.where(offset_lat == HIGH - 2, 1, 0)
        for j in range(WINDOW):
            e = start + j
            center = ext_ref[e]
            packed = jnp.where(from_east, east_ext_ref[e >> 3], west_ext_ref[e >> 3])
            halo = pltpu.roll(packed, (LANES - PITCH * (e & 7)) & (LANES - 1), 1)
            for b in range(4):
                shift = offset_lat - 1 + b
                inside = (lane >= shift) & (lane < LANES + shift)
                shifted_ref[t, b, j] = pltpu.roll(
                    jnp.where(inside, center, halo), (LANES - shift) & (LANES - 1), 1
                )
        for i in range(TILE):
            row = t * TILE + i
            lat_weights = [weights_ref[4 + b, row : row + 1, :] for b in range(4)]
            total = None
            for a in range(4):
                inner = lat_weights[0] * shifted_ref[t, 0, i + a]
                for b in range(1, 4):
                    inner = inner + lat_weights[b] * shifted_ref[t, b, i + a]
                part = weights_ref[a, row : row + 1, :] * inner
                total = part if total is None else total + part
            advected_ref[row] = total

    channel = lax.broadcasted_iota(jnp.int32, (channels, lanes), 0)
    one_lane = lane_iota((1, lanes))
    slots = owner_ref.shape[1]
    capacity = slots // 2
    halves = capacity * FIELD // lanes
    per_row = lanes // FIELD
    sums = [jnp.zeros((channels, lanes), jnp.float32) for _ in range(2 * halves)]
    empty = jnp.where((one_lane & (FIELD - 1)) == channels, jnp.float32(lanes), jnp.float32(0.0))
    places = [empty for _ in range(2 * halves)]
    taken = [jnp.int32(0), jnp.int32(0)]
    for k in range(slots):
        cell = cell_ref[0, k]
        r, c = cell >> 7, cell & (lanes - 1)
        a, b = frac_ref[0, k], frac_ref[1, k]
        near = jnp.where(one_lane == c, 1.0 - b, jnp.where(one_lane == c + 1, b, 0.0))
        value = jnp.sum(
            advected_ref[r] * ((1.0 - a) * near) + advected_ref[r + 1] * (a * near),
            axis=1,
            keepdims=True,
        )
        live = k < count_ref[0, 0]
        side = (owner_ref[0, k] != 0).astype(jnp.int32)
        target = target_ref[0, k].astype(jnp.float32)
        position = jnp.where(side == 0, taken[0], taken[1])
        taken[0] = taken[0] + jnp.where(live & (side == 0), 1, 0)
        taken[1] = taken[1] + jnp.where(live & (side == 1), 1, 0)
        base = (position % per_row) * FIELD
        here = jnp.where(live, side * halves + position // per_row, -1)
        at_value = lane - channel
        for h in range(2 * halves):
            lane_base = jnp.where(here == h, base, -lanes)
            sums[h] = jnp.where(at_value == lane_base, value, sums[h])
            places[h] = jnp.where(one_lane == lane_base + channels, target, places[h])
    lon_count = message_ref.shape[0] // 2
    other = (1 - lax.axis_index("panel")) * lon_count
    message_ref[...] = jnp.zeros_like(message_ref)
    for side in range(2):
        parts = []
        for h in range(halves):
            n = side * halves + h
            parts.append(jnp.sum(sums[n], axis=0, keepdims=True) + places[n])
        message_ref[other + side * (lon_count - 1)] = jnp.concatenate(parts, axis=1)


def column_kernel(advected_ref, out_ref):
    row_count, channels, _ = advected_ref.shape
    for i in range(row_count):
        out_ref[pl.ds(i, channels, stride=row_count), :] = advected_ref[i]


def rim_kernel(received_ref, given_ref, out_ref, rim_ref, sem):
    del given_ref
    channels, row_count, lanes = out_ref.shape
    lon = lax.axis_index("lon")
    lon_count = lax.axis_size("lon")

    @pl.when((lon == 0) | (lon == lon_count - 1))
    def _():
        other = (1 - lax.axis_index("panel")) * lon_count
        values = received_ref[pl.ds(other, lon_count)].reshape(lon_count, received_ref.shape[2])
        lane = lane_iota((lon_count, lanes))
        rim = jnp.zeros((FIELD, lanes), jnp.float32)
        for q in range(received_ref.shape[2] // FIELD):
            entry = values[:, q * FIELD : (q + 1) * FIELD]
            place = entry[:, channels : channels + 1].astype(jnp.int32)
            rim = rim + lax.dot_general(
                entry,
                jnp.where(lane == place, 1.0, 0.0),
                (((0,), (0,)), ((), ())),
                precision=lax.Precision.HIGHEST,
                preferred_element_type=jnp.float32,
            )
        rim_ref[...] = rim[0:channels].reshape(channels, 1, lanes)

        @pl.when(lon == 0)
        def _():
            copy = pltpu.make_async_copy(rim_ref, out_ref.at[:, pl.ds(0, 1), :], sem)
            copy.start()
            copy.wait()

        @pl.when(lon == lon_count - 1)
        def _():
            copy = pltpu.make_async_copy(rim_ref, out_ref.at[:, pl.ds(row_count - 1, 1), :], sem)
            copy.start()
            copy.wait()


def f32(*shape):
    return jax.ShapeDtypeStruct(shape, jnp.float32)


def up(array, axis):
    count = lax.axis_size(axis)
    return lax.ppermute(array, axis, [(i, i + 1) for i in range(count - 1)])


def down(array, axis):
    count = lax.axis_size(axis)
    return lax.ppermute(array, axis, [(i + 1, i) for i in range(count - 1)])


def body(fields, offsets, fractions, send_count, send_owner, send_cell, send_target, send_frac):
    _, channels, row_count, lanes = fields.shape
    groups = row_count // GROUP
    lon_count = lax.axis_size("lon")
    slots = send_owner.shape[-1]
    width = slots // 2 * FIELD
    ext = LOW + row_count + HIGH

    rows, first, last = pl.pallas_call(
        pack_kernel,
        out_shape=(
            f32(row_count, channels, lanes),
            f32(groups, channels, lanes),
            f32(groups, channels, lanes),
        ),
        in_specs=[VMEM],
        out_specs=(VMEM, VMEM, VMEM),
        compiler_params=pltpu.CompilerParams(vmem_limit_bytes=4 * 1024 * 1024),
        name="pack",
    )(fields.reshape(channels * row_count, lanes))
    west = up(last, "lat")
    east = down(first, "lat")
    weights = pl.pallas_call(
        weight_kernel,
        out_shape=f32(8, row_count, lanes),
        in_specs=[VMEM],
        out_specs=VMEM,
        cost_estimate=pl.CostEstimate(flops=200000, bytes_accessed=200000, transcendentals=0),
        compiler_params=pltpu.CompilerParams(vmem_limit_bytes=2 * 1024 * 1024),
        name="weights",
    )(fractions[0])
    to_next, to_prev = pl.pallas_call(
        edge_kernel,
        out_shape=(f32(LOW + 2, channels, lanes), f32(HIGH + 3, channels, lanes)),
        in_specs=[VMEM] * 3,
        out_specs=(VMEM, VMEM),
        compiler_params=pltpu.CompilerParams(vmem_limit_bytes=2 * 1024 * 1024),
        name="edges",
    )(rows, west, east)
    from_prev = up(to_next, "lon")
    from_next = down(to_prev, "lon")
    advected, message = pl.pallas_call(
        advect_kernel,
        out_shape=(f32(row_count, channels, lanes), f32(2 * lon_count, 1, width)),
        in_specs=[SMEM] * 6 + [VMEM] * 6,
        out_specs=(VMEM, VMEM),
        scratch_shapes=[
            pltpu.VMEM((ext, channels, lanes), jnp.float32),
            pltpu.VMEM((groups + 3, channels, lanes), jnp.float32),
            pltpu.VMEM((groups + 3, channels, lanes), jnp.float32),
            pltpu.VMEM((row_count // TILE, 4, WINDOW, channels, lanes), jnp.float32),
        ],
        compiler_params=pltpu.CompilerParams(vmem_limit_bytes=8 * 1024 * 1024),
        name="advect",
    )(
        offsets[0].transpose(0, 2, 1),
        send_count[0],
        send_owner[0, 0],
        send_cell[0, 0],
        send_target[0, 0],
        send_frac[0, 0, 0],
        rows,
        west,
        east,
        from_prev,
        from_next,
        weights,
    )
    received = lax.all_to_all(message, ("panel", "lon"), split_axis=0, concat_axis=0, tiled=True)
    columns = pl.pallas_call(
        column_kernel,
        out_shape=f32(channels * row_count, lanes),
        in_specs=[VMEM],
        out_specs=VMEM,
        cost_estimate=pl.CostEstimate(flops=0, bytes_accessed=2000000, transcendentals=0),
        compiler_params=pltpu.CompilerParams(vmem_limit_bytes=2 * 1024 * 1024),
        name="columns",
    )(advected)
    out = pl.pallas_call(
        rim_kernel,
        out_shape=f32(channels, row_count, lanes),
        in_specs=[VMEM, ANY],
        out_specs=ANY,
        scratch_shapes=[
            pltpu.VMEM((channels, 1, lanes), jnp.float32),
            pltpu.SemaphoreType.DMA(()),
        ],
        input_output_aliases={1: 0},
        compiler_params=pltpu.CompilerParams(vmem_limit_bytes=2 * 1024 * 1024),
        name="rim",
    )(received, columns.reshape(channels, row_count, lanes))
    return out[None]


def solution(mesh):
    placed = (
        P("panel", None, "lon", "lat"),
        P("panel", None, "lon", "lat"),
        P("panel", None, "lon", "lat"),
        P("panel", "lon", "lat"),
        P("panel", "lon", "lat", None),
        P("panel", "lon", "lat", None),
        P("panel", "lon", "lat", None),
        P("panel", "lon", "lat", None, None),
    )
    return jax.shard_map(
        body, mesh=mesh, in_specs=placed, out_specs=P("panel", None, "lon", "lat"), check_vma=False
    )
```

```python
import functools

import jax
import jax.numpy as jnp
from jax import lax
from jax.experimental import pallas as pl
from jax.experimental.pallas import tpu as pltpu
from jax.sharding import PartitionSpec as P

TILE = 8
LOW = 8
HIGH = 9
WINDOW = TILE + 3
LANES = 128
PITCH = 16
GROUP = LANES // PITCH
FIELD = 32

VMEM = pl.BlockSpec(memory_space=pltpu.VMEM)
ANY = pl.BlockSpec(memory_space=pl.ANY)
HBM = pl.BlockSpec(memory_space=pltpu.HBM)


def lane_iota(shape):
    return lax.broadcasted_iota(jnp.int32, shape, len(shape) - 1)


def even_index(axis):
    return lax.axis_index(axis) % 2 == 0


def unpack(west, east, slot):
    lane = lane_iota(west.shape)
    if slot:
        west = pltpu.roll(west, LANES - PITCH * slot, 1)
        east = pltpu.roll(east, LANES - PITCH * slot, 1)
    return jnp.where(lane < LANES // 2, east, west)


def pack_kernel(cells_ref, rows_ref, even_ref, odd_ref, held_ref, sems):
    row_count, channels, lanes = rows_ref.shape
    copies = []
    for m in range(row_count // GROUP):
        part = (slice(None), pl.ds(m * GROUP, GROUP), slice(None))
        copies.append(pltpu.make_async_copy(cells_ref.at[part], held_ref.at[m], sems.at[m]))
        copies[m].start()
    even = even_index("lat")
    lane = lane_iota((channels, lanes))
    for m in range(row_count // GROUP):
        copies[m].wait()
        first = last = None
        for s in range(GROUP):
            row = held_ref[m, :, s, :]
            rows_ref[m * GROUP + s] = row
            turned = row if s == 0 else pltpu.roll(row, PITCH * s, 1)
            if s == 0:
                first = last = turned
            else:
                base = PITCH * s
                first = jnp.where((lane >= base) & (lane < base + HIGH), turned, first)
                last = jnp.where((lane >= base - LOW) & (lane < base), turned, last)
        even_ref[m] = jnp.where(even, last, first)
        odd_ref[m] = jnp.where(even, first, last)


def edge_kernel(rows_ref, even_ref, odd_ref, to_even_ref, to_odd_ref):
    row_count, channels, lanes = rows_ref.shape
    groups = row_count // GROUP
    even_lat, even_lon = even_index("lat"), even_index("lon")
    lane = lane_iota((channels, lanes))
    west = [jnp.where(even_lat, odd_ref[m], even_ref[m]) for m in (0, 1, groups - 1)]
    east = [jnp.where(even_lat, even_ref[m], odd_ref[m]) for m in (0, 1, groups - 1)]
    to_next = [rows_ref[row_count - LOW + i] for i in range(LOW)] + [west[2], east[2]]
    to_prev = [rows_ref[i] for i in range(HIGH)] + [west[0], east[0]]
    to_prev.append(jnp.where(lane < lanes // 2, east[1], west[1]))
    for i, up_row in enumerate(to_prev):
        down_row = to_next[i] if i < len(to_next) else up_row
        to_even_ref[i] = jnp.where(even_lon, down_row, up_row)
        to_odd_ref[i] = jnp.where(even_lon, up_row, down_row)


def prepare_kernel(
    fractions_ref, offsets_ref, count_ref, owner_ref, cell_ref, target_ref, frac_ref,
    even_ref, odd_ref, weights_ref, halo_ref, whole_ref, real_ref,
):
    for axis in range(2):
        x = fractions_ref[axis]
        weights_ref[4 * axis] = -x * (x - 1.0) * (x - 2.0) / 6.0
        weights_ref[4 * axis + 1] = (x + 1.0) * (x - 1.0) * (x - 2.0) / 2.0
        weights_ref[4 * axis + 2] = -(x + 1.0) * x * (x - 2.0) / 2.0
        weights_ref[4 * axis + 3] = (x + 1.0) * x * (x - 1.0) / 6.0
    even = even_index("lat")
    for m in range(halo_ref.shape[0] // GROUP):
        west = jnp.where(even, odd_ref[m], even_ref[m])
        east = jnp.where(even, even_ref[m], odd_ref[m])
        for s in range(GROUP):
            halo_ref[m * GROUP + s] = unpack(west, east, s)
    tiles, slots = offsets_ref.shape[2], owner_ref.shape[1]
    whole_ref[0:1, 0:tiles] = offsets_ref[0]
    whole_ref[1:2, 0:tiles] = offsets_ref[1]
    whole_ref[2:3, 0:1] = count_ref[...]
    whole_ref[3:4, 0:slots] = owner_ref[...]
    whole_ref[4:5, 0:slots] = cell_ref[...]
    whole_ref[5:6, 0:slots] = target_ref[...]
    real_ref[0:2, 0:slots] = frac_ref[...]


def advect_kernel(
    slots, whole_ref, real_ref, rows_ref, halo_ref, weights_ref, even_ref, odd_ref,
    advected_ref, message_ref,
    ext_ref, edge_ref, shifted_ref, ints_ref, frac_ref, sems,
):
    row_count, channels, lanes = rows_ref.shape
    copies = [
        pltpu.make_async_copy(whole_ref, ints_ref, sems.at[0]),
        pltpu.make_async_copy(real_ref, frac_ref, sems.at[1]),
    ]
    for copy in copies:
        copy.start()
    even = even_index("lon")
    prev = [jnp.where(even, odd_ref[i], even_ref[i]) for i in range(LOW + 2)]
    next_ = [jnp.where(even, even_ref[i], odd_ref[i]) for i in range(HIGH + 3)]
    for i in range(LOW):
        ext_ref[i] = prev[i]
        edge_ref[i] = unpack(prev[LOW], prev[LOW + 1], i)
    ext_ref[LOW : LOW + row_count] = rows_ref[...]
    edge_ref[LOW : LOW + row_count] = halo_ref[...]
    for i in range(HIGH):
        ext_ref[LOW + row_count + i] = next_[i]
        packed = (next_[HIGH], next_[HIGH + 1]) if i < GROUP else (next_[HIGH + 2],) * 2
        edge_ref[LOW + row_count + i] = unpack(*packed, i % GROUP)
    for copy in copies:
        copy.wait()

    lane = lane_iota((channels, lanes))
    for t in range(row_count // TILE):
        offset_lat = ints_ref[1, t]
        start = t * TILE + LOW - 1 + ints_ref[0, t]
        for b in range(4):
            shift = offset_lat - 1 + b
            inside = (lane >= shift) & (lane < LANES + shift)
            turn = (LANES - shift) & (LANES - 1)
            for j in range(WINDOW):
                mixed = jnp.where(inside, ext_ref[start + j], edge_ref[start + j])
                shifted_ref[t, b, j] = pltpu.roll(mixed, turn, 1)
        for i in range(TILE):
            row = t * TILE + i
            lat_weights = [weights_ref[4 + b, row : row + 1, :] for b in range(4)]
            total = None
            for a in range(4):
                inner = lat_weights[0] * shifted_ref[t, 0, i + a]
                for b in range(1, 4):
                    inner = inner + lat_weights[b] * shifted_ref[t, b, i + a]
                part = weights_ref[a, row : row + 1, :] * inner
                total = part if total is None else total + part
            advected_ref[row] = total

    channel = lax.broadcasted_iota(jnp.int32, (channels, lanes), 0)
    one_lane = lane_iota((1, lanes))
    capacity = slots // 2
    halves = capacity * FIELD // lanes
    per_row = lanes // FIELD
    sums = [jnp.zeros((channels, lanes), jnp.float32) for _ in range(2 * halves)]
    empty = jnp.where((one_lane & (FIELD - 1)) == channels, jnp.float32(lanes), jnp.float32(0.0))
    places = [empty for _ in range(2 * halves)]
    taken = [jnp.int32(0), jnp.int32(0)]
    at_value = lane - channel
    for k in range(slots):
        cell = ints_ref[4, k]
        r, c = cell >> 7, cell & (lanes - 1)
        a, b = frac_ref[0, k], frac_ref[1, k]
        near = jnp.where(one_lane == c, 1.0 - b, jnp.where(one_lane == c + 1, b, 0.0))
        value = jnp.sum(
            advected_ref[r] * ((1.0 - a) * near) + advected_ref[r + 1] * (a * near),
            axis=1,
            keepdims=True,
        )
        live = k < ints_ref[2, 0]
        side = (ints_ref[3, k] != 0).astype(jnp.int32)
        target = ints_ref[5, k].astype(jnp.float32)
        position = jnp.where(side == 0, taken[0], taken[1])
        taken[0] = taken[0] + jnp.where(live & (side == 0), 1, 0)
        taken[1] = taken[1] + jnp.where(live & (side == 1), 1, 0)
        base = (position % per_row) * FIELD
        here = jnp.where(live, side * halves + position // per_row, -1)
        for h in range(2 * halves):
            lane_base = jnp.where(here == h, base, -lanes)
            sums[h] = jnp.where(at_value == lane_base, value, sums[h])
            places[h] = jnp.where(one_lane == lane_base + channels, target, places[h])
    lon_count = message_ref.shape[0] // (2 * halves)
    other = (1 - lax.axis_index("panel")) * lon_count
    message_ref[...] = jnp.zeros_like(message_ref)
    for side in range(2):
        for h in range(halves):
            n = side * halves + h
            row = (other + side * (lon_count - 1)) * halves + h
            message_ref[pl.ds(row, 1), :] = jnp.sum(sums[n], axis=0, keepdims=True) + places[n]


def column_kernel(advected_ref, out_ref):
    row_count, channels, _ = advected_ref.shape
    for i in range(row_count):
        out_ref[pl.ds(i, channels, stride=row_count), :] = advected_ref[i]


def rim_kernel(lon_count, received_ref, given_ref, out_ref, rim_ref, sem):
    del given_ref
    channels, row_count, lanes = out_ref.shape
    lon = lax.axis_index("lon")

    @pl.when((lon == 0) | (lon == lon_count - 1))
    def _():
        entries = received_ref.shape[0] // 2
        other = (1 - lax.axis_index("panel")) * entries
        values = received_ref[pl.ds(other, entries), :]
        lane = lane_iota((entries, lanes))
        chosen = []
        for q in range(lanes // FIELD):
            at = q * FIELD + channels
            place = values[:, at : at + 1].astype(jnp.int32)
            chosen.append(jnp.where(lane == place, 1.0, 0.0))
        spread = lax.dot_general(
            values,
            jnp.concatenate(chosen, axis=1),
            (((0,), (0,)), ((), ())),
            precision=lax.Precision.HIGHEST,
            preferred_element_type=jnp.float32,
        )
        rim = spread[0:channels, 0:lanes]
        for q in range(1, lanes // FIELD):
            rim = rim + spread[q * FIELD : q * FIELD + channels, q * lanes : (q + 1) * lanes]
        rim_ref[...] = rim.reshape(channels, 1, lanes)
        row = jnp.where(lon == 0, 0, row_count - 1)
        copy = pltpu.make_async_copy(rim_ref, out_ref.at[:, pl.ds(row, 1), :], sem)
        copy.start()
        copy.wait()


def f32(*shape):
    return jax.ShapeDtypeStruct(shape, jnp.float32)


def swap(array, axis, first):
    pairs = []
    for i in range(first, lax.axis_size(axis) - 1, 2):
        pairs += [(i, i + 1), (i + 1, i)]
    return lax.ppermute(array, axis, pairs)


def params(mib):
    return pltpu.CompilerParams(vmem_limit_bytes=mib * 1024 * 1024)


def body(fields, offsets, fractions, send_count, send_owner, send_cell, send_target, send_frac):
    _, channels, row_count, lanes = fields.shape
    groups = row_count // GROUP
    lon_count = lax.axis_size("lon")
    slots = send_owner.shape[-1]
    width = slots // 2 * FIELD
    ext = LOW + row_count + HIGH

    strip = f32(groups, channels, lanes)
    rows, lat_even, lat_odd = pl.pallas_call(
        pack_kernel,
        out_shape=(f32(row_count, channels, lanes), strip, strip),
        in_specs=[HBM],
        out_specs=(VMEM,) * 3,
        scratch_shapes=[
            pltpu.VMEM((groups, channels, GROUP, lanes), jnp.float32),
            pltpu.SemaphoreType.DMA((groups,)),
        ],
        compiler_params=params(4),
        name="pack",
    )(fields[0])
    lat_even = swap(lat_even, "lat", 0)
    lat_odd = swap(lat_odd, "lat", 1)
    edge = f32(HIGH + 3, channels, lanes)
    lon_even, lon_odd = pl.pallas_call(
        edge_kernel,
        out_shape=(edge, edge),
        in_specs=[VMEM] * 3,
        out_specs=(VMEM, VMEM),
        compiler_params=params(2),
        name="edges",
    )(rows, lat_even, lat_odd)
    lon_even = swap(lon_even, "lon", 0)
    lon_odd = swap(lon_odd, "lon", 1)
    weights, halo, whole, real = pl.pallas_call(
        prepare_kernel,
        out_shape=(
            f32(8, row_count, lanes),
            f32(row_count, channels, lanes),
            jax.ShapeDtypeStruct((8, lanes), jnp.int32),
            f32(8, lanes),
        ),
        in_specs=[VMEM] * 9,
        out_specs=(VMEM,) * 4,
        cost_estimate=pl.CostEstimate(flops=400000, bytes_accessed=400000, transcendentals=0),
        compiler_params=params(2),
        name="prepare",
    )(
        fractions[0],
        offsets[0].transpose(0, 2, 1),
        send_count[0],
        send_owner[0, 0],
        send_cell[0, 0],
        send_target[0, 0],
        send_frac[0, 0, 0],
        lat_even,
        lat_odd,
    )
    advected, message = pl.pallas_call(
        functools.partial(advect_kernel, slots),
        out_shape=(
            f32(row_count, channels, lanes),
            f32(2 * lon_count * width // lanes, lanes),
        ),
        in_specs=[VMEM] * 7,
        out_specs=(VMEM, VMEM),
        scratch_shapes=[
            pltpu.VMEM((ext, channels, lanes), jnp.float32),
            pltpu.VMEM((ext, channels, lanes), jnp.float32),
            pltpu.VMEM((row_count // TILE, 4, WINDOW, channels, lanes), jnp.float32),
            pltpu.SMEM((8, lanes), jnp.int32),
            pltpu.SMEM((8, lanes), jnp.float32),
            pltpu.SemaphoreType.DMA((2,)),
        ],
        compiler_params=params(8),
        name="advect",
    )(whole, real, rows, halo, weights, lon_even, lon_odd)
    received = lax.all_to_all(
        message.reshape(2 * lon_count, 1, width), ("panel", "lon"), 0, 0, tiled=True
    )
    columns = pl.pallas_call(
        column_kernel,
        out_shape=f32(channels * row_count, lanes),
        in_specs=[VMEM],
        out_specs=VMEM,
        cost_estimate=pl.CostEstimate(flops=0, bytes_accessed=2000000, transcendentals=0),
        compiler_params=params(2),
        name="columns",
    )(advected)
    out = pl.pallas_call(
        functools.partial(rim_kernel, lon_count),
        out_shape=f32(channels, row_count, lanes),
        in_specs=[VMEM, ANY],
        out_specs=ANY,
        scratch_shapes=[
            pltpu.VMEM((channels, 1, lanes), jnp.float32),
            pltpu.SemaphoreType.DMA(()),
        ],
        input_output_aliases={1: 0},
        compiler_params=params(2),
        name="rim",
    )(received.reshape(message.shape), columns.reshape(channels, row_count, lanes))
    return out[None]


def solution(mesh):
    placed = (
        P("panel", None, "lon", "lat"),
        P("panel", None, "lon", "lat"),
        P("panel", None, "lon", "lat"),
        P("panel", "lon", "lat"),
        P("panel", "lon", "lat", None),
        P("panel", "lon", "lat", None),
        P("panel", "lon", "lat", None),
        P("panel", "lon", "lat", None, None),
    )
    return jax.shard_map(
        body, mesh=mesh, in_specs=placed, out_specs=P("panel", None, "lon", "lat"), check_vma=False
    )
```

```python
import functools

import jax
import jax.numpy as jnp
from jax import lax
from jax.experimental import pallas as pl
from jax.experimental.pallas import tpu as pltpu
from jax.sharding import PartitionSpec as P

TILE = 8
LOW = 8
HIGH = 9
WINDOW = TILE + 3
LANES = 128
PITCH = 8
GROUP = LANES // PITCH
FIRST = {"lon": 1, "lat": 0}
FIELD = 32

VMEM = pl.BlockSpec(memory_space=pltpu.VMEM)
ANY = pl.BlockSpec(memory_space=pl.ANY)
HBM = pl.BlockSpec(memory_space=pltpu.HBM)


def lane_iota(shape):
    return lax.broadcasted_iota(jnp.int32, shape, len(shape) - 1)


def up_first(axis):
    return lax.axis_index(axis) % 2 == FIRST[axis]


def params(mib):
    return pltpu.CompilerParams(vmem_limit_bytes=mib * 1024 * 1024)


def ends_kernel(cells_ref, first_step_ref, second_step_ref, head_ref, tail_ref, ninth_ref, sems):
    row_count = cells_ref.shape[1]
    copies = [
        pltpu.make_async_copy(cells_ref.at[:, 0:LOW, :], head_ref, sems.at[0]),
        pltpu.make_async_copy(cells_ref.at[:, row_count - LOW : row_count, :], tail_ref, sems.at[1]),
        pltpu.make_async_copy(cells_ref.at[:, LOW:HIGH, :], ninth_ref, sems.at[2]),
    ]
    for copy in copies:
        copy.start()
    up = up_first("lon")
    for copy in copies:
        copy.wait()
    for i in range(LOW):
        head, tail = head_ref[:, i, :], tail_ref[:, i, :]
        first_step_ref[i] = jnp.where(up, tail, head)
        second_step_ref[i] = jnp.where(up, head, tail)
    ninth = ninth_ref[:, 0, :]
    first_step_ref[LOW] = ninth
    second_step_ref[LOW] = ninth


def pack(rows, first, last, ninth):
    lane = lane_iota(rows[0][1].shape)
    for e, row in rows:
        g, base = e // GROUP, PITCH * (e % GROUP)
        turned = pltpu.roll(row, base, 1) if base else row
        first[g] = jnp.where((lane >= base) & (lane < base + PITCH), turned, first[g])
        below = (base - PITCH) % LANES
        last[g] = jnp.where((lane >= below) & (lane < below + PITCH), turned, last[g])
        ninth[g] = jnp.where(lane == (base + PITCH) % LANES, turned, ninth[g])


def own_kernel(*refs):
    count_ref, given, outputs, held, sems = refs[0], refs[1:8], refs[8:15], refs[15:22], refs[22]
    rows_ref, first_ref, last_ref, ninth_ref, weights_ref, whole_ref, real_ref = outputs
    fractions_ref, offsets_ref, owner_ref, cell_ref, target_ref, frac_ref, cells_ref = held
    copies = [pltpu.make_async_copy(given[n], held[n], sems.at[n]) for n in range(7)]
    for copy in copies:
        copy.start()
    row_count, channels, lanes = rows_ref.shape
    for copy in copies:
        copy.wait()
    rows = []
    for i in range(row_count):
        row = cells_ref[pl.ds(i, channels, stride=row_count), :]
        rows_ref[i] = row
        rows.append((i + LOW, row))
    empty = jnp.zeros((channels, lanes), jnp.float32)
    first, last, ninth = ([empty] * first_ref.shape[0] for _ in range(3))
    pack(rows, first, last, ninth)
    for g in range(first_ref.shape[0]):
        first_ref[g], last_ref[g], ninth_ref[g] = first[g], last[g], ninth[g]
    for axis in range(2):
        x = fractions_ref[axis]
        weights_ref[4 * axis] = -x * (x - 1.0) * (x - 2.0) / 6.0
        weights_ref[4 * axis + 1] = (x + 1.0) * (x - 1.0) * (x - 2.0) / 2.0
        weights_ref[4 * axis + 2] = -(x + 1.0) * x * (x - 2.0) / 2.0
        weights_ref[4 * axis + 3] = (x + 1.0) * x * (x - 1.0) / 6.0
    tiles, slots = offsets_ref.shape[2], owner_ref.shape[1]
    whole_ref[0:1, 0:tiles] = offsets_ref[0]
    whole_ref[1:2, 0:tiles] = offsets_ref[1]
    whole_ref[2:3, :] = jnp.full((1, lanes), count_ref[0, 0], jnp.int32)
    whole_ref[3:4, 0:slots] = owner_ref[...]
    whole_ref[4:5, 0:slots] = cell_ref[...]
    whole_ref[5:6, 0:slots] = target_ref[...]
    real_ref[0:2, 0:slots] = frac_ref[...]


def sides_kernel(
    from_first_ref, from_second_ref, first_ref, last_ref, ninth_ref, first_step_ref, second_step_ref
):
    groups, channels, lanes = first_ref.shape
    up = up_first("lon")
    prev = [jnp.where(up, from_second_ref[i], from_first_ref[i]) for i in range(LOW)]
    next_ = [jnp.where(up, from_first_ref[i], from_second_ref[i]) for i in range(HIGH)]
    first, last, ninth = ([ref[g] for g in range(groups)] for ref in (first_ref, last_ref, ninth_ref))
    after = groups * GROUP - LOW
    pack([(i, prev[i]) for i in range(LOW)], first, last, ninth)
    pack([(after + i, next_[i]) for i in range(LOW)], first, last, ninth)
    lane = lane_iota((channels, lanes))
    within = lane & (PITCH - 1)
    mixed = ninth[0]
    for g in range(1, groups):
        mixed = jnp.where(within == g, pltpu.roll(ninth[g], g, 1), mixed)
    low_part, high_part = pltpu.roll(next_[LOW], 3, 1), pltpu.roll(next_[LOW], 6, 1)
    mixed = jnp.where((lane >= 3) & (lane < 8), low_part, mixed)
    mixed = jnp.where((lane >= 11) & (lane < 15), high_part, mixed)
    first.append(mixed)
    last.append(next_[LOW])
    up = up_first("lat")
    for g in range(groups + 1):
        first_step_ref[g] = jnp.where(up, last[g], first[g])
        second_step_ref[g] = jnp.where(up, first[g], last[g])


def shift_of(ints_ref, t, b):
    return ints_ref[1, t] - 1 + b


def center_kernel(
    whole_ref, rows_ref, from_first_ref, from_second_ref, centers_ref, ext_ref, ints_ref, sem
):
    row_count, _, _ = rows_ref.shape
    copy = pltpu.make_async_copy(whole_ref, ints_ref, sem)
    copy.start()
    up = up_first("lon")
    for i in range(LOW):
        ext_ref[i] = jnp.where(up, from_second_ref[i], from_first_ref[i])
    ext_ref[LOW : LOW + row_count] = rows_ref[...]
    for i in range(HIGH):
        ext_ref[LOW + row_count + i] = jnp.where(up, from_first_ref[i], from_second_ref[i])
    copy.wait()
    for t in range(row_count // TILE):
        start = t * TILE + LOW - 1 + ints_ref[0, t]
        for b in range(4):
            turn = (LANES - shift_of(ints_ref, t, b)) & (LANES - 1)
            for j in range(WINDOW):
                centers_ref[t, b, j] = pltpu.roll(ext_ref[start + j], turn, 1)


def advect_kernel(
    slots, whole_ref, real_ref, centers_ref, weights_ref, from_first_ref, from_second_ref,
    advected_ref, message_ref,
    east_ref, west_ref, ninth_ref, shifted_ref, ints_ref, frac_ref, sems,
):
    row_count, channels, lanes = advected_ref.shape
    copies = [
        pltpu.make_async_copy(whole_ref, ints_ref, sems.at[0]),
        pltpu.make_async_copy(real_ref, frac_ref, sems.at[1]),
    ]
    for copy in copies:
        copy.start()
    lane = lane_iota((channels, lanes))
    up = up_first("lat")
    groups = east_ref.shape[0] - 1
    for g in range(groups + 1):
        west_ref[g] = jnp.where(up, from_second_ref[g], from_first_ref[g])
    for g in range(groups):
        east_ref[g] = jnp.where(up, from_first_ref[g], from_second_ref[g])
    mixed = jnp.where(up, from_first_ref[groups], from_second_ref[groups])
    ninth_ref[0] = mixed
    for g in range(1, groups):
        ninth_ref[g] = pltpu.roll(mixed, LANES - g, 1)
    last_row = jnp.where(lane < 5, pltpu.roll(mixed, LANES - 3, 1), pltpu.roll(mixed, LANES - 6, 1))
    east_ref[groups] = last_row
    ninth_ref[groups] = last_row
    for copy in copies:
        copy.wait()

    within = lane & (PITCH - 1)
    for t in range(row_count // TILE):
        offset_lat = ints_ref[1, t]
        start = t * TILE + LOW - 1 + ints_ref[0, t]
        from_east = within < offset_lat + 2
        for j in range(WINDOW):
            e = start + j
            g, base = e >> 4, PITCH * (e & (GROUP - 1))
            packed = jnp.where(from_east, east_ref[g], west_ref[g])
            beyond = jnp.where(offset_lat + 2 == HIGH, (base + PITCH) & (LANES - 1), -1)
            for b in range(4):
                shift = shift_of(ints_ref, t, b)
                inside = (lane >= -shift) & (lane < LANES - shift)
                if b == 3:
                    packed = jnp.where(lane == beyond, ninth_ref[g], packed)
                halo = pltpu.roll(packed, (2 * LANES - base - shift) & (LANES - 1), 1)
                shifted_ref[t, b, j] = jnp.where(inside, centers_ref[t, b, j], halo)
    for t in range(row_count // TILE):
        for i in range(TILE):
            row = t * TILE + i
            lat_weights = [weights_ref[4 + b, row : row + 1, :] for b in range(4)]
            total = None
            for a in range(4):
                inner = lat_weights[0] * shifted_ref[t, 0, i + a]
                for b in range(1, 4):
                    inner = inner + lat_weights[b] * shifted_ref[t, b, i + a]
                part = weights_ref[a, row : row + 1, :] * inner
                total = part if total is None else total + part
            advected_ref[row] = total

    channel = lax.broadcasted_iota(jnp.int32, (channels, lanes), 0)
    one_lane = lane_iota((1, lanes))
    capacity = slots // 2
    halves = capacity * FIELD // lanes
    per_row = lanes // FIELD
    sums = [jnp.zeros((channels, lanes), jnp.float32) for _ in range(2 * halves)]
    empty = jnp.where((one_lane & (FIELD - 1)) == channels, jnp.float32(lanes), jnp.float32(0.0))
    places = [empty for _ in range(2 * halves)]
    taken = [jnp.int32(0), jnp.int32(0)]
    at_value = lane - channel
    for k in range(slots):
        cell = ints_ref[4, k]
        r, c = cell >> 7, cell & (lanes - 1)
        a, b = frac_ref[0, k], frac_ref[1, k]
        near = jnp.where(one_lane == c, 1.0 - b, jnp.where(one_lane == c + 1, b, 0.0))
        value = jnp.sum(
            advected_ref[r] * ((1.0 - a) * near) + advected_ref[r + 1] * (a * near),
            axis=1,
            keepdims=True,
        )
        live = k < ints_ref[2, 0]
        side = (ints_ref[3, k] != 0).astype(jnp.int32)
        target = ints_ref[5, k].astype(jnp.float32)
        position = jnp.where(side == 0, taken[0], taken[1])
        taken[0] = taken[0] + jnp.where(live & (side == 0), 1, 0)
        taken[1] = taken[1] + jnp.where(live & (side == 1), 1, 0)
        base = (position % per_row) * FIELD
        here = jnp.where(live, side * halves + position // per_row, -1)
        for h in range(2 * halves):
            lane_base = jnp.where(here == h, base, -lanes)
            sums[h] = jnp.where(at_value == lane_base, value, sums[h])
            places[h] = jnp.where(one_lane == lane_base + channels, target, places[h])
    lon_count = message_ref.shape[0] // (2 * halves)
    other = (1 - lax.axis_index("panel")) * lon_count
    message_ref[...] = jnp.zeros_like(message_ref)
    for side in range(2):
        for h in range(halves):
            n = side * halves + h
            row = (other + side * (lon_count - 1)) * halves + h
            message_ref[pl.ds(row, 1), :] = jnp.sum(sums[n], axis=0, keepdims=True) + places[n]


def column_kernel(advected_ref, out_ref):
    row_count, channels, _ = advected_ref.shape
    for i in range(row_count):
        out_ref[pl.ds(i, channels, stride=row_count), :] = advected_ref[i]


def rim_kernel(lon_count, received_ref, given_ref, out_ref, rim_ref, sem):
    del given_ref
    channels, row_count, lanes = out_ref.shape
    lon = lax.axis_index("lon")

    @pl.when((lon == 0) | (lon == lon_count - 1))
    def _():
        entries = received_ref.shape[0] // 2
        other = (1 - lax.axis_index("panel")) * entries
        values = received_ref[pl.ds(other, entries), :]
        lane = lane_iota((entries, lanes))
        chosen = []
        for q in range(lanes // FIELD):
            at = q * FIELD + channels
            place = values[:, at : at + 1].astype(jnp.int32)
            chosen.append(jnp.where(lane == place, 1.0, 0.0))
        spread = lax.dot_general(
            values,
            jnp.concatenate(chosen, axis=1),
            (((0,), (0,)), ((), ())),
            precision=lax.Precision.HIGHEST,
            preferred_element_type=jnp.float32,
        )
        rim = spread[0:channels, 0:lanes]
        for q in range(1, lanes // FIELD):
            rim = rim + spread[q * FIELD : q * FIELD + channels, q * lanes : (q + 1) * lanes]
        rim_ref[...] = rim.reshape(channels, 1, lanes)
        row = jnp.where(lon == 0, 0, row_count - 1)
        copy = pltpu.make_async_copy(rim_ref, out_ref.at[:, pl.ds(row, 1), :], sem)
        copy.start()
        copy.wait()


def f32(*shape):
    return jax.ShapeDtypeStruct(shape, jnp.float32)


def swap(array, axis, first):
    pairs = []
    for i in range(first, lax.axis_size(axis) - 1, 2):
        pairs += [(i, i + 1), (i + 1, i)]
    return lax.ppermute(array, axis, pairs)


def body(fields, offsets, fractions, send_count, send_owner, send_cell, send_target, send_frac):
    _, channels, row_count, lanes = fields.shape
    groups = (LOW + row_count + LOW) // GROUP
    tiles = row_count // TILE
    lon_count = lax.axis_size("lon")
    slots = send_owner.shape[-1]
    width = slots // 2 * FIELD
    ext = LOW + row_count + HIGH

    ends = f32(HIGH, channels, lanes)
    lon_first, lon_second = pl.pallas_call(
        ends_kernel,
        out_shape=(ends, ends),
        in_specs=[HBM],
        out_specs=(VMEM, VMEM),
        scratch_shapes=[
            pltpu.VMEM((channels, LOW, lanes), jnp.float32),
            pltpu.VMEM((channels, LOW, lanes), jnp.float32),
            pltpu.VMEM((channels, HIGH - LOW, lanes), jnp.float32),
            pltpu.SemaphoreType.DMA((3,)),
        ],
        compiler_params=params(2),
        name="ends",
    )(pltpu.with_memory_space_constraint(fields[0], pltpu.HBM))
    lon_first = swap(lon_first, "lon", FIRST["lon"])
    lon_second = swap(lon_second, "lon", 1 - FIRST["lon"])
    arguments = (
        fractions[0],
        offsets[0].transpose(0, 2, 1),
        send_owner[0, 0],
        send_cell[0, 0],
        send_target[0, 0],
        send_frac[0, 0, 0],
        fields.reshape(channels * row_count, lanes),
    )
    part = f32(groups, channels, lanes)
    rows, first, last, ninth, weights, whole, real = pl.pallas_call(
        own_kernel,
        out_shape=(
            f32(row_count, channels, lanes),
            part,
            part,
            part,
            f32(8, row_count, lanes),
            jax.ShapeDtypeStruct((8, lanes), jnp.int32),
            f32(8, lanes),
        ),
        in_specs=[pl.BlockSpec(memory_space=pltpu.SMEM)] + [HBM] * 7,
        out_specs=(VMEM,) * 7,
        scratch_shapes=[pltpu.VMEM(given.shape, given.dtype) for given in arguments]
        + [pltpu.SemaphoreType.DMA((7,))],
        cost_estimate=pl.CostEstimate(flops=400000, bytes_accessed=800000, transcendentals=0),
        compiler_params=params(4),
        name="own",
    )(send_count[0], *[pltpu.with_memory_space_constraint(given, pltpu.HBM) for given in arguments])
    strips = f32(groups + 1, channels, lanes)
    lat_first, lat_second = pl.pallas_call(
        sides_kernel,
        out_shape=(strips, strips),
        in_specs=[VMEM] * 5,
        out_specs=(VMEM, VMEM),
        compiler_params=params(2),
        name="sides",
    )(lon_first, lon_second, first, last, ninth)
    lat_first = swap(lat_first, "lat", FIRST["lat"])
    lat_second = swap(lat_second, "lat", 1 - FIRST["lat"])
    centers = pl.pallas_call(
        center_kernel,
        out_shape=f32(tiles, 4, WINDOW, channels, lanes),
        in_specs=[VMEM] * 4,
        out_specs=VMEM,
        scratch_shapes=[
            pltpu.VMEM((ext, channels, lanes), jnp.float32),
            pltpu.SMEM((8, lanes), jnp.int32),
            pltpu.SemaphoreType.DMA(()),
        ],
        cost_estimate=pl.CostEstimate(flops=400000, bytes_accessed=3000000, transcendentals=0),
        compiler_params=params(4),
        name="centers",
    )(whole, rows, lon_first, lon_second)
    advected, message = pl.pallas_call(
        functools.partial(advect_kernel, slots),
        out_shape=(
            f32(row_count, channels, lanes),
            f32(2 * lon_count * width // lanes, lanes),
        ),
        in_specs=[VMEM] * 6,
        out_specs=(VMEM, VMEM),
        scratch_shapes=[
            pltpu.VMEM((groups + 1, channels, lanes), jnp.float32),
            pltpu.VMEM((groups + 1, channels, lanes), jnp.float32),
            pltpu.VMEM((groups + 1, channels, lanes), jnp.float32),
            pltpu.VMEM((tiles, 4, WINDOW, channels, lanes), jnp.float32),
            pltpu.SMEM((8, lanes), jnp.int32),
            pltpu.SMEM((8, lanes), jnp.float32),
            pltpu.SemaphoreType.DMA((2,)),
        ],
        compiler_params=params(8),
        name="advect",
    )(whole, real, centers, weights, lat_first, lat_second)
    received = lax.all_to_all(
        message.reshape(2 * lon_count, 1, width), ("panel", "lon"), 0, 0, tiled=True
    )
    columns = pl.pallas_call(
        column_kernel,
        out_shape=f32(channels * row_count, lanes),
        in_specs=[VMEM],
        out_specs=VMEM,
        cost_estimate=pl.CostEstimate(flops=0, bytes_accessed=2000000, transcendentals=0),
        compiler_params=params(2),
        name="columns",
    )(advected)
    out = pl.pallas_call(
        functools.partial(rim_kernel, lon_count),
        out_shape=f32(channels, row_count, lanes),
        in_specs=[VMEM, ANY],
        out_specs=ANY,
        scratch_shapes=[
            pltpu.VMEM((channels, 1, lanes), jnp.float32),
            pltpu.SemaphoreType.DMA(()),
        ],
        input_output_aliases={1: 0},
        compiler_params=params(2),
        name="rim",
    )(received.reshape(message.shape), columns.reshape(channels, row_count, lanes))
    return out[None]


def solution(mesh):
    placed = (
        P("panel", None, "lon", "lat"),
        P("panel", None, "lon", "lat"),
        P("panel", None, "lon", "lat"),
        P("panel", "lon", "lat"),
        P("panel", "lon", "lat", None),
        P("panel", "lon", "lat", None),
        P("panel", "lon", "lat", None),
        P("panel", "lon", "lat", None, None),
    )
    return jax.shard_map(
        body, mesh=mesh, in_specs=placed, out_specs=P("panel", None, "lon", "lat"), check_vma=False
    )
```

```python
import functools

import jax
import jax.numpy as jnp
from jax import lax
from jax.experimental import pallas as pl
from jax.experimental.pallas import tpu as pltpu
from jax.sharding import PartitionSpec as P

TILE = 8
LOW = 8
HIGH = 9
WINDOW = TILE + 3
LANES = 128
PITCH = 8
GROUP = LANES // PITCH
FIRST = {"lon": 1, "lat": 0}
ROOT = (1, 20)
FIELD = 32

VMEM = pl.BlockSpec(memory_space=pltpu.VMEM)
ANY = pl.BlockSpec(memory_space=pl.ANY)
HBM = pl.BlockSpec(memory_space=pltpu.HBM)
SMEM = pl.BlockSpec(memory_space=pltpu.SMEM)


def lane_iota(shape):
    return lax.broadcasted_iota(jnp.int32, shape, len(shape) - 1)


def place_of(panel, lon, lon_count):
    return (panel ^ ROOT[0]) * lon_count + (lon + lon_count - ROOT[1] % lon_count) % lon_count


def placed_in(array, space):
    return pltpu.with_memory_space_constraint(array, space)


def up_first(axis):
    return lax.axis_index(axis) % 2 == FIRST[axis]


def params(mib):
    return pltpu.CompilerParams(vmem_limit_bytes=mib * 1024 * 1024)


def ends_kernel(cells_ref, first_step_ref, second_step_ref, head_ref, tail_ref, ninth_ref, sems):
    row_count = cells_ref.shape[1]
    copies = [
        pltpu.make_async_copy(cells_ref.at[:, 0:LOW, :], head_ref, sems.at[0]),
        pltpu.make_async_copy(cells_ref.at[:, row_count - LOW : row_count, :], tail_ref, sems.at[1]),
        pltpu.make_async_copy(cells_ref.at[:, LOW:HIGH, :], ninth_ref, sems.at[2]),
    ]
    for copy in copies:
        copy.start()
    up = up_first("lon")
    for copy in copies:
        copy.wait()
    for i in range(LOW):
        head, tail = head_ref[:, i, :], tail_ref[:, i, :]
        first_step_ref[i] = jnp.where(up, tail, head)
        second_step_ref[i] = jnp.where(up, head, tail)
    ninth = ninth_ref[:, 0, :]
    first_step_ref[LOW] = ninth
    second_step_ref[LOW] = ninth


def pack(rows, first, last, ninth):
    lane = lane_iota(rows[0][1].shape)
    for e, row in rows:
        g, base = e // GROUP, PITCH * (e % GROUP)
        turned = pltpu.roll(row, base, 1) if base else row
        first[g] = jnp.where((lane >= base) & (lane < base + PITCH), turned, first[g])
        below = (base - PITCH) % LANES
        last[g] = jnp.where((lane >= below) & (lane < below + PITCH), turned, last[g])
        ninth[g] = jnp.where(lane == (base + PITCH) % LANES, turned, ninth[g])


def own_kernel(
    count_ref, fractions_in, cells_in, offsets_in, owner_in, cell_in, target_in, frac_in,
    rows_ref, first_ref, last_ref, ninth_ref, weights_ref,
    count_out, offsets_out, owner_out, cell_out, target_out, frac_out,
    fractions_ref, cells_ref, sems,
):
    moves = (
        (cells_in, cells_ref),
        (fractions_in, fractions_ref),
        (offsets_in, offsets_out),
        (owner_in, owner_out),
        (cell_in, cell_out),
        (target_in, target_out),
        (frac_in, frac_out),
    )
    copies = [pltpu.make_async_copy(*move, sems.at[n]) for n, move in enumerate(moves)]
    for copy in copies:
        copy.start()
    count_out[0, 0] = count_ref[0, 0]
    row_count, channels, lanes = rows_ref.shape
    copies[0].wait()
    rows = []
    for i in range(row_count):
        row = cells_ref[pl.ds(i, channels, stride=row_count), :]
        rows_ref[i] = row
        rows.append((i + LOW, row))
    empty = jnp.zeros((channels, lanes), jnp.float32)
    first, last, ninth = ([empty] * first_ref.shape[0] for _ in range(3))
    pack(rows, first, last, ninth)
    for g in range(first_ref.shape[0]):
        first_ref[g], last_ref[g], ninth_ref[g] = first[g], last[g], ninth[g]
    copies[1].wait()
    for axis in range(2):
        x = fractions_ref[axis]
        weights_ref[4 * axis] = -x * (x - 1.0) * (x - 2.0) / 6.0
        weights_ref[4 * axis + 1] = (x + 1.0) * (x - 1.0) * (x - 2.0) / 2.0
        weights_ref[4 * axis + 2] = -(x + 1.0) * x * (x - 2.0) / 2.0
        weights_ref[4 * axis + 3] = (x + 1.0) * x * (x - 1.0) / 6.0
    for copy in copies[2:]:
        copy.wait()


def sides_kernel(
    from_first_ref, from_second_ref, first_ref, last_ref, ninth_ref, first_step_ref, second_step_ref
):
    groups, channels, lanes = first_ref.shape
    up = up_first("lon")
    prev = [jnp.where(up, from_second_ref[i], from_first_ref[i]) for i in range(LOW)]
    next_ = [jnp.where(up, from_first_ref[i], from_second_ref[i]) for i in range(HIGH)]
    first, last, ninth = ([ref[g] for g in range(groups)] for ref in (first_ref, last_ref, ninth_ref))
    after = groups * GROUP - LOW
    pack([(i, prev[i]) for i in range(LOW)], first, last, ninth)
    pack([(after + i, next_[i]) for i in range(LOW)], first, last, ninth)
    lane = lane_iota((channels, lanes))
    within = lane & (PITCH - 1)
    mixed = ninth[0]
    for g in range(1, groups):
        mixed = jnp.where(within == g, pltpu.roll(ninth[g], g, 1), mixed)
    low_part, high_part = pltpu.roll(next_[LOW], 3, 1), pltpu.roll(next_[LOW], 6, 1)
    mixed = jnp.where((lane >= 3) & (lane < 8), low_part, mixed)
    mixed = jnp.where((lane >= 11) & (lane < 15), high_part, mixed)
    first.append(mixed)
    last.append(next_[LOW])
    up = up_first("lat")
    for g in range(groups + 1):
        first_step_ref[g] = jnp.where(up, last[g], first[g])
        second_step_ref[g] = jnp.where(up, first[g], last[g])


def shift_of(offsets_ref, t, b):
    return offsets_ref[1, 0, t] - 1 + b


def center_kernel(
    offsets_ref, rows_ref, from_first_ref, from_second_ref, centers_ref, ext_ref
):
    row_count, _, _ = rows_ref.shape
    up = up_first("lon")
    for i in range(LOW):
        ext_ref[i] = jnp.where(up, from_second_ref[i], from_first_ref[i])
    ext_ref[LOW : LOW + row_count] = rows_ref[...]
    for i in range(HIGH):
        ext_ref[LOW + row_count + i] = jnp.where(up, from_first_ref[i], from_second_ref[i])
    for t in range(row_count // TILE):
        start = t * TILE + LOW - 1 + offsets_ref[0, 0, t]
        for b in range(4):
            turn = (LANES - shift_of(offsets_ref, t, b)) & (LANES - 1)
            for j in range(WINDOW):
                centers_ref[t, b, j] = pltpu.roll(ext_ref[start + j], turn, 1)


def advect_kernel(
    count_ref, offsets_ref, owner_ref, cell_ref, target_ref, frac_ref, centers_ref, weights_ref, from_first_ref, from_second_ref,
    advected_ref, message_ref,
    east_ref, west_ref, ninth_ref, shifted_ref,
):
    row_count, channels, lanes = advected_ref.shape
    slots = owner_ref.shape[1]
    lane = lane_iota((channels, lanes))
    up = up_first("lat")
    groups = east_ref.shape[0] - 1
    for g in range(groups + 1):
        west_ref[g] = jnp.where(up, from_second_ref[g], from_first_ref[g])
    for g in range(groups):
        east_ref[g] = jnp.where(up, from_first_ref[g], from_second_ref[g])
    mixed = jnp.where(up, from_first_ref[groups], from_second_ref[groups])
    ninth_ref[0] = mixed
    for g in range(1, groups):
        ninth_ref[g] = pltpu.roll(mixed, LANES - g, 1)
    last_row = jnp.where(lane < 5, pltpu.roll(mixed, LANES - 3, 1), pltpu.roll(mixed, LANES - 6, 1))
    east_ref[groups] = last_row
    ninth_ref[groups] = last_row

    within = lane & (PITCH - 1)
    for t in range(row_count // TILE):
        offset_lat = offsets_ref[1, 0, t]
        start = t * TILE + LOW - 1 + offsets_ref[0, 0, t]
        from_east = within < offset_lat + 2
        for j in range(WINDOW):
            e = start + j
            g, base = e >> 4, PITCH * (e & (GROUP - 1))
            packed = jnp.where(from_east, east_ref[g], west_ref[g])
            beyond = jnp.where(offset_lat + 2 == HIGH, (base + PITCH) & (LANES - 1), -1)
            for b in range(4):
                shift = shift_of(offsets_ref, t, b)
                inside = (lane >= -shift) & (lane < LANES - shift)
                if b == 3:
                    packed = jnp.where(lane == beyond, ninth_ref[g], packed)
                halo = pltpu.roll(packed, (2 * LANES - base - shift) & (LANES - 1), 1)
                shifted_ref[t, b, j] = jnp.where(inside, centers_ref[t, b, j], halo)
    for t in range(row_count // TILE):
        for i in range(TILE):
            row = t * TILE + i
            lat_weights = [weights_ref[4 + b, row : row + 1, :] for b in range(4)]
            total = None
            for a in range(4):
                inner = lat_weights[0] * shifted_ref[t, 0, i + a]
                for b in range(1, 4):
                    inner = inner + lat_weights[b] * shifted_ref[t, b, i + a]
                part = weights_ref[a, row : row + 1, :] * inner
                total = part if total is None else total + part
            advected_ref[row] = total

    channel = lax.broadcasted_iota(jnp.int32, (channels, lanes), 0)
    one_lane = lane_iota((1, lanes))
    capacity = slots // 2
    halves = capacity * FIELD // lanes
    per_row = lanes // FIELD
    sums = [jnp.zeros((channels, lanes), jnp.float32) for _ in range(2 * halves)]
    empty = jnp.where((one_lane & (FIELD - 1)) == channels, jnp.float32(lanes), jnp.float32(0.0))
    places = [empty for _ in range(2 * halves)]
    taken = [jnp.int32(0), jnp.int32(0)]
    at_value = lane - channel
    for k in range(slots):
        cell = cell_ref[0, k]
        r, c = cell >> 7, cell & (lanes - 1)
        a, b = frac_ref[0, k], frac_ref[1, k]
        near = jnp.where(one_lane == c, 1.0 - b, jnp.where(one_lane == c + 1, b, 0.0))
        value = jnp.sum(
            advected_ref[r] * ((1.0 - a) * near) + advected_ref[r + 1] * (a * near),
            axis=1,
            keepdims=True,
        )
        live = k < count_ref[0, 0]
        side = (owner_ref[0, k] != 0).astype(jnp.int32)
        target = target_ref[0, k].astype(jnp.float32)
        position = jnp.where(side == 0, taken[0], taken[1])
        taken[0] = taken[0] + jnp.where(live & (side == 0), 1, 0)
        taken[1] = taken[1] + jnp.where(live & (side == 1), 1, 0)
        base = (position % per_row) * FIELD
        here = jnp.where(live, side * halves + position // per_row, -1)
        for h in range(2 * halves):
            lane_base = jnp.where(here == h, base, -lanes)
            sums[h] = jnp.where(at_value == lane_base, value, sums[h])
            places[h] = jnp.where(one_lane == lane_base + channels, target, places[h])
    lon_count = message_ref.shape[0] // (2 * halves)
    other = 1 - lax.axis_index("panel")
    message_ref[...] = jnp.zeros_like(message_ref)
    for side in range(2):
        for h in range(halves):
            n = side * halves + h
            row = place_of(other, side * (lon_count - 1), lon_count) * halves + h
            message_ref[pl.ds(row, 1), :] = jnp.sum(sums[n], axis=0, keepdims=True) + places[n]


def column_kernel(advected_ref, out_ref):
    row_count, channels, _ = advected_ref.shape
    for i in range(row_count):
        out_ref[pl.ds(i, channels, stride=row_count), :] = advected_ref[i]


def rim_kernel(lon_count, received_ref, given_ref, out_ref, rim_ref, sem):
    del given_ref
    channels, row_count, lanes = out_ref.shape
    lon = lax.axis_index("lon")

    @pl.when((lon == 0) | (lon == lon_count - 1))
    def _():
        entries = received_ref.shape[0] // 2
        other = (1 - lax.axis_index("panel")) ^ ROOT[0]
        values = received_ref[pl.ds(other * entries, entries), :]
        lane = lane_iota((entries, lanes))
        chosen = []
        for q in range(lanes // FIELD):
            at = q * FIELD + channels
            place = values[:, at : at + 1].astype(jnp.int32)
            chosen.append(jnp.where(lane == place, 1.0, 0.0))
        spread = lax.dot_general(
            values,
            jnp.concatenate(chosen, axis=1),
            (((0,), (0,)), ((), ())),
            precision=lax.Precision.HIGHEST,
            preferred_element_type=jnp.float32,
        )
        rim = spread[0:channels, 0:lanes]
        for q in range(1, lanes // FIELD):
            rim = rim + spread[q * FIELD : q * FIELD + channels, q * lanes : (q + 1) * lanes]
        rim_ref[...] = rim.reshape(channels, 1, lanes)
        row = jnp.where(lon == 0, 0, row_count - 1)
        copy = pltpu.make_async_copy(rim_ref, out_ref.at[:, pl.ds(row, 1), :], sem)
        copy.start()
        copy.wait()


def f32(*shape):
    return jax.ShapeDtypeStruct(shape, jnp.float32)


def swap(array, axis, first):
    pairs = []
    for i in range(first, lax.axis_size(axis) - 1, 2):
        pairs += [(i, i + 1), (i + 1, i)]
    return lax.ppermute(array, axis, pairs)


def body(fields, offsets, fractions, send_count, send_owner, send_cell, send_target, send_frac):
    _, channels, row_count, lanes = fields.shape
    groups = (LOW + row_count + LOW) // GROUP
    tiles = row_count // TILE
    lon_count = lax.axis_size("lon")
    slots = send_owner.shape[-1]
    width = slots // 2 * FIELD
    ext = LOW + row_count + HIGH

    ends = f32(HIGH, channels, lanes)
    lon_first, lon_second = pl.pallas_call(
        ends_kernel,
        out_shape=(ends, ends),
        in_specs=[HBM],
        out_specs=(VMEM, VMEM),
        scratch_shapes=[
            pltpu.VMEM((channels, LOW, lanes), jnp.float32),
            pltpu.VMEM((channels, LOW, lanes), jnp.float32),
            pltpu.VMEM((channels, HIGH - LOW, lanes), jnp.float32),
            pltpu.SemaphoreType.DMA((3,)),
        ],
        compiler_params=params(2),
        name="ends",
    )(placed_in(fields[0], pltpu.HBM))
    lon_first = swap(lon_first, "lon", FIRST["lon"])
    lon_second = swap(lon_second, "lon", 1 - FIRST["lon"])
    small = (
        offsets[0].transpose(0, 2, 1),
        send_owner[0, 0],
        send_cell[0, 0],
        send_target[0, 0],
        send_frac[0, 0, 0],
    )
    large = (fractions[0], fields.reshape(channels * row_count, lanes))
    part = f32(groups, channels, lanes)
    rows, first, last, ninth, weights, *small = pl.pallas_call(
        own_kernel,
        out_shape=(
            f32(row_count, channels, lanes),
            part,
            part,
            part,
            f32(8, row_count, lanes),
            *(pltpu.SMEM(given.shape, given.dtype) for given in (send_count[0], *small)),
        ),
        in_specs=[SMEM] + [HBM] * 7,
        out_specs=(VMEM,) * 5 + (SMEM,) * 6,
        scratch_shapes=[pltpu.VMEM(given.shape, given.dtype) for given in large]
        + [pltpu.SemaphoreType.DMA((7,))],
        cost_estimate=pl.CostEstimate(flops=400000, bytes_accessed=800000, transcendentals=0),
        compiler_params=params(4),
        name="own",
    )(send_count[0], *(placed_in(given, pltpu.HBM) for given in large + small))
    small = [placed_in(given, pltpu.SMEM) for given in small]
    strips = f32(groups + 1, channels, lanes)
    lat_first, lat_second = pl.pallas_call(
        sides_kernel,
        out_shape=(strips, strips),
        in_specs=[VMEM] * 5,
        out_specs=(VMEM, VMEM),
        compiler_params=params(2),
        name="sides",
    )(lon_first, lon_second, first, last, ninth)
    lat_first = swap(lat_first, "lat", FIRST["lat"])
    lat_second = swap(lat_second, "lat", 1 - FIRST["lat"])
    centers = pl.pallas_call(
        center_kernel,
        out_shape=f32(tiles, 4, WINDOW, channels, lanes),
        in_specs=[SMEM] + [VMEM] * 3,
        out_specs=VMEM,
        scratch_shapes=[pltpu.VMEM((ext, channels, lanes), jnp.float32)],
        cost_estimate=pl.CostEstimate(flops=400000, bytes_accessed=3000000, transcendentals=0),
        compiler_params=params(4),
        name="centers",
    )(small[1], rows, lon_first, lon_second)
    advected, message = pl.pallas_call(
        advect_kernel,
        out_shape=(
            f32(row_count, channels, lanes),
            f32(2 * lon_count * width // lanes, lanes),
        ),
        in_specs=[SMEM] * 6 + [VMEM] * 4,
        out_specs=(VMEM, VMEM),
        scratch_shapes=[
            pltpu.VMEM((groups + 1, channels, lanes), jnp.float32),
            pltpu.VMEM((groups + 1, channels, lanes), jnp.float32),
            pltpu.VMEM((groups + 1, channels, lanes), jnp.float32),
            pltpu.VMEM((tiles, 4, WINDOW, channels, lanes), jnp.float32),
        ],
        compiler_params=params(8),
        name="advect",
    )(*small, centers, weights, lat_first, lat_second)
    group = [0] * (2 * lon_count)
    for panel in range(2):
        for lon in range(lon_count):
            group[place_of(panel, lon, lon_count)] = panel * lon_count + lon
    received = lax.all_to_all(
        message.reshape(2 * lon_count, 1, width),
        ("panel", "lon"),
        0,
        0,
        tiled=True,
        axis_index_groups=[group],
    )
    columns = pl.pallas_call(
        column_kernel,
        out_shape=f32(channels * row_count, lanes),
        in_specs=[VMEM],
        out_specs=VMEM,
        cost_estimate=pl.CostEstimate(flops=0, bytes_accessed=2000000, transcendentals=0),
        compiler_params=params(2),
        name="columns",
    )(advected)
    out = pl.pallas_call(
        functools.partial(rim_kernel, lon_count),
        out_shape=f32(channels, row_count, lanes),
        in_specs=[VMEM, ANY],
        out_specs=ANY,
        scratch_shapes=[
            pltpu.VMEM((channels, 1, lanes), jnp.float32),
            pltpu.SemaphoreType.DMA(()),
        ],
        input_output_aliases={1: 0},
        compiler_params=params(2),
        name="rim",
    )(received.reshape(message.shape), columns.reshape(channels, row_count, lanes))
    return out[None]


def solution(mesh):
    placed = (
        P("panel", None, "lon", "lat"),
        P("panel", None, "lon", "lat"),
        P("panel", None, "lon", "lat"),
        P("panel", "lon", "lat"),
        P("panel", "lon", "lat", None),
        P("panel", "lon", "lat", None),
        P("panel", "lon", "lat", None),
        P("panel", "lon", "lat", None, None),
    )
    return jax.shard_map(
        body, mesh=mesh, in_specs=placed, out_specs=P("panel", None, "lon", "lat"), check_vma=False
    )
```

```python
import functools

import jax
import jax.numpy as jnp
from jax import lax
from jax.experimental import pallas as pl
from jax.experimental.pallas import tpu as pltpu
from jax.sharding import PartitionSpec as P

TILE = 8
LOW = 8
HIGH = 9
WINDOW = TILE + 3
LANES = 128
PITCH = 8
GROUP = LANES // PITCH
FIRST = {"lon": 1, "lat": 0}
ROOT = (1, 20)
FIELD = 32

VMEM = pl.BlockSpec(memory_space=pltpu.VMEM)
ANY = pl.BlockSpec(memory_space=pl.ANY)
HBM = pl.BlockSpec(memory_space=pltpu.HBM)
SMEM = pl.BlockSpec(memory_space=pltpu.SMEM)


def lane_iota(shape):
    return lax.broadcasted_iota(jnp.int32, shape, len(shape) - 1)


def place_of(panel, lon, lon_count):
    return (panel ^ ROOT[0]) * lon_count + (lon + lon_count - ROOT[1] % lon_count) % lon_count


def placed_in(array, space):
    return pltpu.with_memory_space_constraint(array, space)


def up_first(axis):
    return lax.axis_index(axis) % 2 == FIRST[axis]


def params(mib):
    return pltpu.CompilerParams(vmem_limit_bytes=mib * 1024 * 1024)


def ends_kernel(cells_ref, first_step_ref, second_step_ref, head_ref, tail_ref, ninth_ref, sems):
    row_count = cells_ref.shape[1]
    copies = [
        pltpu.make_async_copy(cells_ref.at[:, 0:LOW, :], head_ref, sems.at[0]),
        pltpu.make_async_copy(cells_ref.at[:, row_count - LOW : row_count, :], tail_ref, sems.at[1]),
        pltpu.make_async_copy(cells_ref.at[:, LOW:HIGH, :], ninth_ref, sems.at[2]),
    ]
    for copy in copies:
        copy.start()
    up = up_first("lon")
    for copy in copies:
        copy.wait()
    for i in range(LOW):
        head, tail = head_ref[:, i, :], tail_ref[:, i, :]
        first_step_ref[i] = jnp.where(up, tail, head)
        second_step_ref[i] = jnp.where(up, head, tail)
    ninth = ninth_ref[:, 0, :]
    first_step_ref[LOW] = ninth
    second_step_ref[LOW] = ninth


def pack(rows, first, last, ninth):
    lane = lane_iota(rows[0][1].shape)
    for e, row in rows:
        g, base = e // GROUP, PITCH * (e % GROUP)
        turned = pltpu.roll(row, base, 1) if base else row
        first[g] = jnp.where((lane >= base) & (lane < base + PITCH), turned, first[g])
        below = (base - PITCH) % LANES
        last[g] = jnp.where((lane >= below) & (lane < below + PITCH), turned, last[g])
        ninth[g] = jnp.where(lane == (base + PITCH) % LANES, turned, ninth[g])


def own_kernel(
    count_ref, fractions_in, cells_in, offsets_in, owner_in, cell_in, target_in, frac_in,
    rows_ref, first_ref, last_ref, ninth_ref, weights_ref,
    count_out, offsets_out, owner_out, cell_out, target_out, frac_out,
    fractions_ref, cells_ref, sems,
):
    moves = (
        (cells_in, cells_ref),
        (fractions_in, fractions_ref),
        (offsets_in, offsets_out),
        (owner_in, owner_out),
        (cell_in, cell_out),
        (target_in, target_out),
        (frac_in, frac_out),
    )
    copies = [pltpu.make_async_copy(*move, sems.at[n]) for n, move in enumerate(moves)]
    for copy in copies:
        copy.start()
    count_out[0, 0] = count_ref[0, 0]
    row_count, channels, lanes = rows_ref.shape
    copies[0].wait()
    rows = []
    for i in range(row_count):
        row = cells_ref[pl.ds(i, channels, stride=row_count), :]
        rows_ref[i] = row
        rows.append((i + LOW, row))
    empty = jnp.zeros((channels, lanes), jnp.float32)
    first, last, ninth = ([empty] * first_ref.shape[0] for _ in range(3))
    pack(rows, first, last, ninth)
    for g in range(first_ref.shape[0]):
        first_ref[g], last_ref[g], ninth_ref[g] = first[g], last[g], ninth[g]
    copies[1].wait()
    for axis in range(2):
        x = fractions_ref[axis]
        weights_ref[4 * axis] = -x * (x - 1.0) * (x - 2.0) / 6.0
        weights_ref[4 * axis + 1] = (x + 1.0) * (x - 1.0) * (x - 2.0) / 2.0
        weights_ref[4 * axis + 2] = -(x + 1.0) * x * (x - 2.0) / 2.0
        weights_ref[4 * axis + 3] = (x + 1.0) * x * (x - 1.0) / 6.0
    for copy in copies[2:]:
        copy.wait()


def sides_kernel(
    from_first_ref, from_second_ref, first_ref, last_ref, ninth_ref, first_step_ref, second_step_ref
):
    groups, channels, lanes = first_ref.shape
    up = up_first("lon")
    prev = [jnp.where(up, from_second_ref[i], from_first_ref[i]) for i in range(LOW)]
    next_ = [jnp.where(up, from_first_ref[i], from_second_ref[i]) for i in range(HIGH)]
    first, last, ninth = ([ref[g] for g in range(groups)] for ref in (first_ref, last_ref, ninth_ref))
    after = groups * GROUP - LOW
    pack([(i, prev[i]) for i in range(LOW)], first, last, ninth)
    pack([(after + i, next_[i]) for i in range(LOW)], first, last, ninth)
    lane = lane_iota((channels, lanes))
    within = lane & (PITCH - 1)
    mixed = ninth[0]
    for g in range(1, groups):
        mixed = jnp.where(within == g, pltpu.roll(ninth[g], g, 1), mixed)
    low_part, high_part = pltpu.roll(next_[LOW], 3, 1), pltpu.roll(next_[LOW], 6, 1)
    mixed = jnp.where((lane >= 3) & (lane < 8), low_part, mixed)
    mixed = jnp.where((lane >= 11) & (lane < 15), high_part, mixed)
    first.append(mixed)
    last.append(next_[LOW])
    up = up_first("lat")
    for g in range(groups + 1):
        first_step_ref[g] = jnp.where(up, last[g], first[g])
        second_step_ref[g] = jnp.where(up, first[g], last[g])


def shift_of(offsets_ref, t, b):
    return offsets_ref[1, 0, t] - 1 + b


def center_kernel(
    offsets_ref, rows_ref, from_first_ref, from_second_ref, centers_ref, ext_ref
):
    row_count, _, _ = rows_ref.shape
    up = up_first("lon")
    for i in range(LOW):
        ext_ref[i] = jnp.where(up, from_second_ref[i], from_first_ref[i])
    ext_ref[LOW : LOW + row_count] = rows_ref[...]
    for i in range(HIGH):
        ext_ref[LOW + row_count + i] = jnp.where(up, from_first_ref[i], from_second_ref[i])
    for t in range(row_count // TILE):
        start = t * TILE + LOW - 1 + offsets_ref[0, 0, t]
        for b in range(4):
            turn = (LANES - shift_of(offsets_ref, t, b)) & (LANES - 1)
            for j in range(WINDOW):
                centers_ref[t, b, j] = pltpu.roll(ext_ref[start + j], turn, 1)


def advect_kernel(
    count_ref, offsets_ref, owner_ref, cell_ref, target_ref, frac_ref, centers_ref, weights_ref, from_first_ref, from_second_ref,
    columns_ref, message_ref,
    advected_ref, east_ref, west_ref, ninth_ref, shifted_ref,
):
    row_count, channels, lanes = advected_ref.shape
    slots = owner_ref.shape[1]
    lane = lane_iota((channels, lanes))
    up = up_first("lat")
    groups = east_ref.shape[0] - 1
    for g in range(groups + 1):
        west_ref[g] = jnp.where(up, from_second_ref[g], from_first_ref[g])
    for g in range(groups):
        east_ref[g] = jnp.where(up, from_first_ref[g], from_second_ref[g])
    mixed = jnp.where(up, from_first_ref[groups], from_second_ref[groups])
    ninth_ref[0] = mixed
    for g in range(1, groups):
        ninth_ref[g] = pltpu.roll(mixed, LANES - g, 1)
    last_row = jnp.where(lane < 5, pltpu.roll(mixed, LANES - 3, 1), pltpu.roll(mixed, LANES - 6, 1))
    east_ref[groups] = last_row
    ninth_ref[groups] = last_row

    within = lane & (PITCH - 1)
    for t in range(row_count // TILE):
        offset_lat = offsets_ref[1, 0, t]
        start = t * TILE + LOW - 1 + offsets_ref[0, 0, t]
        from_east = within < offset_lat + 2
        for j in range(WINDOW):
            e = start + j
            g, base = e >> 4, PITCH * (e & (GROUP - 1))
            packed = jnp.where(from_east, east_ref[g], west_ref[g])
            beyond = jnp.where(offset_lat + 2 == HIGH, (base + PITCH) & (LANES - 1), -1)
            for b in range(4):
                shift = shift_of(offsets_ref, t, b)
                inside = (lane >= -shift) & (lane < LANES - shift)
                if b == 3:
                    packed = jnp.where(lane == beyond, ninth_ref[g], packed)
                halo = pltpu.roll(packed, (2 * LANES - base - shift) & (LANES - 1), 1)
                shifted_ref[t, b, j] = jnp.where(inside, centers_ref[t, b, j], halo)
    for t in range(row_count // TILE):
        for i in range(TILE):
            row = t * TILE + i
            lat_weights = [weights_ref[4 + b, row : row + 1, :] for b in range(4)]
            total = None
            for a in range(4):
                inner = lat_weights[0] * shifted_ref[t, 0, i + a]
                for b in range(1, 4):
                    inner = inner + lat_weights[b] * shifted_ref[t, b, i + a]
                part = weights_ref[a, row : row + 1, :] * inner
                total = part if total is None else total + part
            advected_ref[row] = total
            columns_ref[pl.ds(row, channels, stride=row_count), :] = total

    channel = lax.broadcasted_iota(jnp.int32, (channels, lanes), 0)
    one_lane = lane_iota((1, lanes))
    capacity = slots // 2
    halves = capacity * FIELD // lanes
    per_row = lanes // FIELD
    sums = [jnp.zeros((channels, lanes), jnp.float32) for _ in range(2 * halves)]
    empty = jnp.where((one_lane & (FIELD - 1)) == channels, jnp.float32(lanes), jnp.float32(0.0))
    places = [empty for _ in range(2 * halves)]
    taken = [jnp.int32(0), jnp.int32(0)]
    at_value = lane - channel
    for k in range(slots):
        cell = cell_ref[0, k]
        r, c = cell >> 7, cell & (lanes - 1)
        a, b = frac_ref[0, k], frac_ref[1, k]
        near = jnp.where(one_lane == c, 1.0 - b, jnp.where(one_lane == c + 1, b, 0.0))
        value = jnp.sum(
            advected_ref[r] * ((1.0 - a) * near) + advected_ref[r + 1] * (a * near),
            axis=1,
            keepdims=True,
        )
        live = k < count_ref[0, 0]
        side = (owner_ref[0, k] != 0).astype(jnp.int32)
        target = target_ref[0, k].astype(jnp.float32)
        position = jnp.where(side == 0, taken[0], taken[1])
        taken[0] = taken[0] + jnp.where(live & (side == 0), 1, 0)
        taken[1] = taken[1] + jnp.where(live & (side == 1), 1, 0)
        base = (position % per_row) * FIELD
        here = jnp.where(live, side * halves + position // per_row, -1)
        for h in range(2 * halves):
            lane_base = jnp.where(here == h, base, -lanes)
            sums[h] = jnp.where(at_value == lane_base, value, sums[h])
            places[h] = jnp.where(one_lane == lane_base + channels, target, places[h])
    lon_count = message_ref.shape[0] // (2 * halves)
    other = 1 - lax.axis_index("panel")
    message_ref[...] = jnp.zeros_like(message_ref)
    for side in range(2):
        for h in range(halves):
            n = side * halves + h
            row = place_of(other, side * (lon_count - 1), lon_count) * halves + h
            message_ref[pl.ds(row, 1), :] = jnp.sum(sums[n], axis=0, keepdims=True) + places[n]


def finish_kernel(lon_count, received_ref, columns_ref, out_ref, held_ref, sems):
    channels, row_count, lanes = out_ref.shape
    tiles = row_count // TILE
    lon = lax.axis_index("lon")

    def tile_of(ref, t):
        return ref.at[:, pl.ds(pl.multiple_of(t * TILE, TILE), TILE), :]

    changed = jnp.where(lon == 0, 0, tiles - 1)
    copies = []
    for n in range(tiles - 1):
        t = n + jnp.where(lon == 0, 1, 0)
        copies.append(
            pltpu.make_async_copy(tile_of(columns_ref, t), tile_of(out_ref, t), sems.at[n])
        )
        copies[n].start()
    held_ref[...] = columns_ref[:, pl.ds(pl.multiple_of(changed * TILE, TILE), TILE), :]

    @pl.when((lon == 0) | (lon == lon_count - 1))
    def _():
        entries = received_ref.shape[0] // 2
        other = (1 - lax.axis_index("panel")) ^ ROOT[0]
        values = received_ref[pl.ds(other * entries, entries), :]
        lane = lane_iota((entries, lanes))
        chosen = []
        for q in range(lanes // FIELD):
            at = q * FIELD + channels
            place = values[:, at : at + 1].astype(jnp.int32)
            chosen.append(jnp.where(lane == place, 1.0, 0.0))
        spread = lax.dot_general(
            values,
            jnp.concatenate(chosen, axis=1),
            (((0,), (0,)), ((), ())),
            precision=lax.Precision.HIGHEST,
            preferred_element_type=jnp.float32,
        )
        rim = spread[0:channels, 0:lanes]
        for q in range(1, lanes // FIELD):
            rim = rim + spread[q * FIELD : q * FIELD + channels, q * lanes : (q + 1) * lanes]
        row = jnp.where(lon == 0, 0, TILE - 1)
        held_ref[:, pl.ds(row, 1), :] = rim.reshape(channels, 1, lanes)

    copies.append(pltpu.make_async_copy(held_ref, tile_of(out_ref, changed), sems.at[tiles - 1]))
    copies[tiles - 1].start()
    for copy in copies:
        copy.wait()


def f32(*shape):
    return jax.ShapeDtypeStruct(shape, jnp.float32)


def swap(array, axis, first):
    pairs = []
    for i in range(first, lax.axis_size(axis) - 1, 2):
        pairs += [(i, i + 1), (i + 1, i)]
    return lax.ppermute(array, axis, pairs)


def body(fields, offsets, fractions, send_count, send_owner, send_cell, send_target, send_frac):
    _, channels, row_count, lanes = fields.shape
    groups = (LOW + row_count + LOW) // GROUP
    tiles = row_count // TILE
    lon_count = lax.axis_size("lon")
    slots = send_owner.shape[-1]
    width = slots // 2 * FIELD
    ext = LOW + row_count + HIGH

    ends = f32(HIGH, channels, lanes)
    lon_first, lon_second = pl.pallas_call(
        ends_kernel,
        out_shape=(ends, ends),
        in_specs=[HBM],
        out_specs=(VMEM, VMEM),
        scratch_shapes=[
            pltpu.VMEM((channels, LOW, lanes), jnp.float32),
            pltpu.VMEM((channels, LOW, lanes), jnp.float32),
            pltpu.VMEM((channels, HIGH - LOW, lanes), jnp.float32),
            pltpu.SemaphoreType.DMA((3,)),
        ],
        compiler_params=params(2),
        name="ends",
    )(placed_in(fields[0], pltpu.HBM))
    lon_first = swap(lon_first, "lon", FIRST["lon"])
    lon_second = swap(lon_second, "lon", 1 - FIRST["lon"])
    small = (
        offsets[0].transpose(0, 2, 1),
        send_owner[0, 0],
        send_cell[0, 0],
        send_target[0, 0],
        send_frac[0, 0, 0],
    )
    large = (fractions[0], fields.reshape(channels * row_count, lanes))
    part = f32(groups, channels, lanes)
    rows, first, last, ninth, weights, *small = pl.pallas_call(
        own_kernel,
        out_shape=(
            f32(row_count, channels, lanes),
            part,
            part,
            part,
            f32(8, row_count, lanes),
            *(pltpu.SMEM(given.shape, given.dtype) for given in (send_count[0], *small)),
        ),
        in_specs=[SMEM] + [HBM] * 7,
        out_specs=(VMEM,) * 5 + (SMEM,) * 6,
        scratch_shapes=[pltpu.VMEM(given.shape, given.dtype) for given in large]
        + [pltpu.SemaphoreType.DMA((7,))],
        cost_estimate=pl.CostEstimate(flops=400000, bytes_accessed=800000, transcendentals=0),
        compiler_params=params(4),
        name="own",
    )(send_count[0], *(placed_in(given, pltpu.HBM) for given in large + small))
    small = [placed_in(given, pltpu.SMEM) for given in small]
    strips = f32(groups + 1, channels, lanes)
    lat_first, lat_second = pl.pallas_call(
        sides_kernel,
        out_shape=(strips, strips),
        in_specs=[VMEM] * 5,
        out_specs=(VMEM, VMEM),
        compiler_params=params(2),
        name="sides",
    )(lon_first, lon_second, first, last, ninth)
    lat_first = swap(lat_first, "lat", FIRST["lat"])
    lat_second = swap(lat_second, "lat", 1 - FIRST["lat"])
    centers = pl.pallas_call(
        center_kernel,
        out_shape=f32(tiles, 4, WINDOW, channels, lanes),
        in_specs=[SMEM] + [VMEM] * 3,
        out_specs=VMEM,
        scratch_shapes=[pltpu.VMEM((ext, channels, lanes), jnp.float32)],
        cost_estimate=pl.CostEstimate(flops=400000, bytes_accessed=3000000, transcendentals=0),
        compiler_params=params(4),
        name="centers",
    )(small[1], rows, lon_first, lon_second)
    columns, message = pl.pallas_call(
        advect_kernel,
        out_shape=(
            pltpu.VMEM((channels * row_count, lanes), jnp.float32),
            f32(2 * lon_count * width // lanes, lanes),
        ),
        in_specs=[SMEM] * 6 + [VMEM] * 4,
        out_specs=(VMEM, VMEM),
        scratch_shapes=[
            pltpu.VMEM((row_count, channels, lanes), jnp.float32),
            pltpu.VMEM((groups + 1, channels, lanes), jnp.float32),
            pltpu.VMEM((groups + 1, channels, lanes), jnp.float32),
            pltpu.VMEM((groups + 1, channels, lanes), jnp.float32),
            pltpu.VMEM((tiles, 4, WINDOW, channels, lanes), jnp.float32),
        ],
        compiler_params=params(8),
        name="advect",
    )(*small, centers, weights, lat_first, lat_second)
    group = [0] * (2 * lon_count)
    for panel in range(2):
        for lon in range(lon_count):
            group[place_of(panel, lon, lon_count)] = panel * lon_count + lon
    received = lax.all_to_all(
        message.reshape(2 * lon_count, 1, width),
        ("panel", "lon"),
        0,
        0,
        tiled=True,
        axis_index_groups=[group],
    )
    out = pl.pallas_call(
        functools.partial(finish_kernel, lon_count),
        out_shape=pltpu.HBM((channels, row_count, lanes), jnp.float32),
        in_specs=[VMEM, VMEM],
        out_specs=HBM,
        scratch_shapes=[
            pltpu.VMEM((channels, TILE, lanes), jnp.float32),
            pltpu.SemaphoreType.DMA((tiles,)),
        ],
        compiler_params=params(2),
        name="finish",
    )(received.reshape(message.shape), columns.reshape(channels, row_count, lanes))
    return out[None]


def solution(mesh):
    placed = (
        P("panel", None, "lon", "lat"),
        P("panel", None, "lon", "lat"),
        P("panel", None, "lon", "lat"),
        P("panel", "lon", "lat"),
        P("panel", "lon", "lat", None),
        P("panel", "lon", "lat", None),
        P("panel", "lon", "lat", None),
        P("panel", "lon", "lat", None, None),
    )
    return jax.shard_map(
        body, mesh=mesh, in_specs=placed, out_specs=P("panel", None, "lon", "lat"), check_vma=False
    )
```

```python
import functools

import jax
import jax.numpy as jnp
from jax import lax
from jax.experimental import pallas as pl
from jax.experimental.pallas import tpu as pltpu
from jax.sharding import PartitionSpec as P

TILE = 8
LOW = 8
HIGH = 9
WINDOW = TILE + 3
LANES = 128
PITCH = 8
GROUP = LANES // PITCH
FIRST = {"lon": 1, "lat": 0}
ROOT = (1, 20)
FIELD = 32

VMEM = pl.BlockSpec(memory_space=pltpu.VMEM)
ANY = pl.BlockSpec(memory_space=pl.ANY)
HBM = pl.BlockSpec(memory_space=pltpu.HBM)
SMEM = pl.BlockSpec(memory_space=pltpu.SMEM)


def lane_iota(shape):
    return lax.broadcasted_iota(jnp.int32, shape, len(shape) - 1)


def place_of(panel, lon, lon_count):
    return (panel ^ ROOT[0]) * lon_count + (lon + lon_count - ROOT[1] % lon_count) % lon_count


def placed_in(array, space):
    return pltpu.with_memory_space_constraint(array, space)


def up_first(axis):
    return lax.axis_index(axis) % 2 == FIRST[axis]


def params(mib):
    return pltpu.CompilerParams(vmem_limit_bytes=mib * 1024 * 1024)


def ends_kernel(cells_ref, first_step_ref, second_step_ref, sems):
    row_count = cells_ref.shape[1]
    up = up_first("lon")
    copies = []
    for step, out_ref in enumerate((first_step_ref, second_step_ref)):
        upward = up if step == 0 else jnp.logical_not(up)
        for i in range(HIGH):
            row = jnp.where(upward, min(row_count - LOW + i, row_count - 1), i)
            copies.append(
                pltpu.make_async_copy(cells_ref.at[:, row, :], out_ref.at[i], sems.at[step, i])
            )
            copies[-1].start()
    for copy in copies:
        copy.wait()


def pack(rows, first, last, ninth):
    lane = lane_iota(rows[0][1].shape)
    for e, row in rows:
        g, base = e // GROUP, PITCH * (e % GROUP)
        turned = pltpu.roll(row, base, 1) if base else row
        first[g] = jnp.where((lane >= base) & (lane < base + PITCH), turned, first[g])
        below = (base - PITCH) % LANES
        last[g] = jnp.where((lane >= below) & (lane < below + PITCH), turned, last[g])
        ninth[g] = jnp.where(lane == (base + PITCH) % LANES, turned, ninth[g])


def own_kernel(
    count_ref, fractions_in, cells_in, offsets_in, owner_in, cell_in, target_in, frac_in,
    rows_ref, first_ref, last_ref, ninth_ref, weights_ref,
    count_out, offsets_out, owner_out, cell_out, target_out, frac_out,
    fractions_ref, cells_ref, sems,
):
    moves = (
        (cells_in, cells_ref),
        (fractions_in, fractions_ref),
        (offsets_in, offsets_out),
        (owner_in, owner_out),
        (cell_in, cell_out),
        (target_in, target_out),
        (frac_in, frac_out),
    )
    copies = [pltpu.make_async_copy(*move, sems.at[n]) for n, move in enumerate(moves)]
    for copy in copies:
        copy.start()
    count_out[0, 0] = count_ref[0, 0]
    row_count, channels, lanes = rows_ref.shape
    copies[0].wait()
    rows = []
    for i in range(row_count):
        row = cells_ref[pl.ds(i, channels, stride=row_count), :]
        rows_ref[i] = row
        rows.append((i + LOW, row))
    empty = jnp.zeros((channels, lanes), jnp.float32)
    first, last, ninth = ([empty] * first_ref.shape[0] for _ in range(3))
    pack(rows, first, last, ninth)
    for g in range(first_ref.shape[0]):
        first_ref[g], last_ref[g], ninth_ref[g] = first[g], last[g], ninth[g]
    copies[1].wait()
    for axis in range(2):
        x = fractions_ref[axis]
        weights_ref[4 * axis] = -x * (x - 1.0) * (x - 2.0) / 6.0
        weights_ref[4 * axis + 1] = (x + 1.0) * (x - 1.0) * (x - 2.0) / 2.0
        weights_ref[4 * axis + 2] = -(x + 1.0) * x * (x - 2.0) / 2.0
        weights_ref[4 * axis + 3] = (x + 1.0) * x * (x - 1.0) / 6.0
    for copy in copies[2:]:
        copy.wait()


def sides_kernel(
    from_first_ref, from_second_ref, first_ref, last_ref, ninth_ref, first_step_ref, second_step_ref
):
    groups, channels, lanes = first_ref.shape
    up = up_first("lon")
    prev = [jnp.where(up, from_second_ref[i], from_first_ref[i]) for i in range(LOW)]
    next_ = [jnp.where(up, from_first_ref[i], from_second_ref[i]) for i in range(HIGH)]
    first, last, ninth = ([ref[g] for g in range(groups)] for ref in (first_ref, last_ref, ninth_ref))
    after = groups * GROUP - LOW
    pack([(i, prev[i]) for i in range(LOW)], first, last, ninth)
    pack([(after + i, next_[i]) for i in range(LOW)], first, last, ninth)
    lane = lane_iota((channels, lanes))
    within = lane & (PITCH - 1)
    mixed = ninth[0]
    for g in range(1, groups):
        mixed = jnp.where(within == g, pltpu.roll(ninth[g], g, 1), mixed)
    low_part, high_part = pltpu.roll(next_[LOW], 3, 1), pltpu.roll(next_[LOW], 6, 1)
    mixed = jnp.where((lane >= 3) & (lane < 8), low_part, mixed)
    mixed = jnp.where((lane >= 11) & (lane < 15), high_part, mixed)
    first.append(mixed)
    last.append(next_[LOW])
    up = up_first("lat")
    for g in range(groups + 1):
        first_step_ref[g] = jnp.where(up, last[g], first[g])
        second_step_ref[g] = jnp.where(up, first[g], last[g])


def shift_of(offsets_ref, t, b):
    return offsets_ref[1, 0, t] - 1 + b


def center_kernel(
    offsets_ref, rows_ref, from_first_ref, from_second_ref, centers_ref, ext_ref
):
    row_count, _, _ = rows_ref.shape
    up = up_first("lon")
    for i in range(LOW):
        ext_ref[i] = jnp.where(up, from_second_ref[i], from_first_ref[i])
    ext_ref[LOW : LOW + row_count] = rows_ref[...]
    for i in range(HIGH):
        ext_ref[LOW + row_count + i] = jnp.where(up, from_first_ref[i], from_second_ref[i])
    for t in range(row_count // TILE):
        start = t * TILE + LOW - 1 + offsets_ref[0, 0, t]
        for b in range(4):
            turn = (LANES - shift_of(offsets_ref, t, b)) & (LANES - 1)
            for j in range(WINDOW):
                centers_ref[t, b, j] = pltpu.roll(ext_ref[start + j], turn, 1)


def advect_kernel(
    count_ref, offsets_ref, owner_ref, cell_ref, target_ref, frac_ref, centers_ref, weights_ref, from_first_ref, from_second_ref,
    columns_ref, message_ref,
    advected_ref, east_ref, west_ref, ninth_ref,
):
    row_count, channels, lanes = advected_ref.shape
    slots = owner_ref.shape[1]
    lane = lane_iota((channels, lanes))
    up = up_first("lat")
    groups = east_ref.shape[0] - 1
    for g in range(groups + 1):
        west_ref[g] = jnp.where(up, from_second_ref[g], from_first_ref[g])
    for g in range(groups):
        east_ref[g] = jnp.where(up, from_first_ref[g], from_second_ref[g])
    mixed = jnp.where(up, from_first_ref[groups], from_second_ref[groups])
    ninth_ref[0] = mixed
    for g in range(1, groups):
        ninth_ref[g] = pltpu.roll(mixed, LANES - g, 1)
    last_row = jnp.where(lane < 5, pltpu.roll(mixed, LANES - 3, 1), pltpu.roll(mixed, LANES - 6, 1))
    east_ref[groups] = last_row
    ninth_ref[groups] = last_row

    within = lane & (PITCH - 1)
    for t in range(row_count // TILE):
        offset_lat = offsets_ref[1, 0, t]
        start = t * TILE + LOW - 1 + offsets_ref[0, 0, t]
        from_east = within < offset_lat + 2
        weights, sums = {}, {}
        for j in range(WINDOW):
            e = start + j
            g, base = e >> 4, PITCH * (e & (GROUP - 1))
            packed = jnp.where(from_east, east_ref[g], west_ref[g])
            beyond = jnp.where(offset_lat + 2 == HIGH, (base + PITCH) & (LANES - 1), -1)
            shifted = []
            for b in range(4):
                shift = shift_of(offsets_ref, t, b)
                inside = (lane >= -shift) & (lane < LANES - shift)
                if b == 3:
                    packed = jnp.where(lane == beyond, ninth_ref[g], packed)
                halo = pltpu.roll(packed, (2 * LANES - base - shift) & (LANES - 1), 1)
                shifted.append(jnp.where(inside, centers_ref[t, b, j], halo))
            for i in range(max(j - 3, 0), min(j, TILE - 1) + 1):
                row, a = t * TILE + i, j - i
                if a == 0:
                    weights[i] = [weights_ref[4 + b, row : row + 1, :] for b in range(4)]
                inner = weights[i][0] * shifted[0]
                for b in range(1, 4):
                    inner = inner + weights[i][b] * shifted[b]
                part = weights_ref[a, row : row + 1, :] * inner
                sums[i] = part if a == 0 else sums[i] + part
                if a == 3:
                    advected_ref[row] = sums[i]
                    columns_ref[pl.ds(row, channels, stride=row_count), :] = sums[i]

    channel = lax.broadcasted_iota(jnp.int32, (channels, lanes), 0)
    one_lane = lane_iota((1, lanes))
    capacity = slots // 2
    halves = capacity * FIELD // lanes
    per_row = lanes // FIELD
    sums = [jnp.zeros((channels, lanes), jnp.float32) for _ in range(2 * halves)]
    empty = jnp.where((one_lane & (FIELD - 1)) == channels, jnp.float32(lanes), jnp.float32(0.0))
    places = [empty for _ in range(2 * halves)]
    taken = [jnp.int32(0), jnp.int32(0)]
    at_value = lane - channel
    for k in range(slots):
        cell = cell_ref[0, k]
        r, c = cell >> 7, cell & (lanes - 1)
        a, b = frac_ref[0, k], frac_ref[1, k]
        near = jnp.where(one_lane == c, 1.0 - b, jnp.where(one_lane == c + 1, b, 0.0))
        value = jnp.sum(
            advected_ref[r] * ((1.0 - a) * near) + advected_ref[r + 1] * (a * near),
            axis=1,
            keepdims=True,
        )
        live = k < count_ref[0, 0]
        side = (owner_ref[0, k] != 0).astype(jnp.int32)
        target = target_ref[0, k].astype(jnp.float32)
        position = jnp.where(side == 0, taken[0], taken[1])
        taken[0] = taken[0] + jnp.where(live & (side == 0), 1, 0)
        taken[1] = taken[1] + jnp.where(live & (side == 1), 1, 0)
        base = (position % per_row) * FIELD
        here = jnp.where(live, side * halves + position // per_row, -1)
        for h in range(2 * halves):
            lane_base = jnp.where(here == h, base, -lanes)
            sums[h] = jnp.where(at_value == lane_base, value, sums[h])
            places[h] = jnp.where(one_lane == lane_base + channels, target, places[h])
    lon_count = message_ref.shape[0] // (2 * halves)
    other = 1 - lax.axis_index("panel")
    message_ref[...] = jnp.zeros_like(message_ref)
    for side in range(2):
        for h in range(halves):
            n = side * halves + h
            row = place_of(other, side * (lon_count - 1), lon_count) * halves + h
            message_ref[pl.ds(row, 1), :] = jnp.sum(sums[n], axis=0, keepdims=True) + places[n]


def finish_kernel(lon_count, received_ref, columns_ref, out_ref, held_ref, sems):
    channels, row_count, lanes = out_ref.shape
    tiles = row_count // TILE
    lon = lax.axis_index("lon")

    def tile_of(ref, t):
        return ref.at[:, pl.ds(pl.multiple_of(t * TILE, TILE), TILE), :]

    changed = jnp.where(lon == 0, 0, tiles - 1)
    copies = []
    for n in range(tiles - 1):
        t = n + jnp.where(lon == 0, 1, 0)
        copies.append(
            pltpu.make_async_copy(tile_of(columns_ref, t), tile_of(out_ref, t), sems.at[n])
        )
        copies[n].start()
    held_ref[...] = columns_ref[:, pl.ds(pl.multiple_of(changed * TILE, TILE), TILE), :]

    @pl.when((lon == 0) | (lon == lon_count - 1))
    def _():
        entries = received_ref.shape[0] // 2
        other = (1 - lax.axis_index("panel")) ^ ROOT[0]
        values = received_ref[pl.ds(other * entries, entries), :]
        lane = lane_iota((entries, lanes))
        chosen = []
        for q in range(lanes // FIELD):
            at = q * FIELD + channels
            place = values[:, at : at + 1].astype(jnp.int32)
            chosen.append(jnp.where(lane == place, 1.0, 0.0))
        spread = lax.dot_general(
            values,
            jnp.concatenate(chosen, axis=1),
            (((0,), (0,)), ((), ())),
            precision=lax.Precision.HIGHEST,
            preferred_element_type=jnp.float32,
        )
        rim = spread[0:channels, 0:lanes]
        for q in range(1, lanes // FIELD):
            rim = rim + spread[q * FIELD : q * FIELD + channels, q * lanes : (q + 1) * lanes]
        row = jnp.where(lon == 0, 0, TILE - 1)
        held_ref[:, pl.ds(row, 1), :] = rim.reshape(channels, 1, lanes)

    copies.append(pltpu.make_async_copy(held_ref, tile_of(out_ref, changed), sems.at[tiles - 1]))
    copies[tiles - 1].start()
    for copy in copies:
        copy.wait()


def f32(*shape):
    return jax.ShapeDtypeStruct(shape, jnp.float32)


def swap(array, axis, first):
    pairs = []
    for i in range(first, lax.axis_size(axis) - 1, 2):
        pairs += [(i, i + 1), (i + 1, i)]
    return lax.ppermute(array, axis, pairs)


def body(fields, offsets, fractions, send_count, send_owner, send_cell, send_target, send_frac):
    _, channels, row_count, lanes = fields.shape
    groups = (LOW + row_count + LOW) // GROUP
    tiles = row_count // TILE
    lon_count = lax.axis_size("lon")
    slots = send_owner.shape[-1]
    width = slots // 2 * FIELD
    ext = LOW + row_count + HIGH

    ends = f32(HIGH, channels, lanes)
    lon_first, lon_second = pl.pallas_call(
        ends_kernel,
        out_shape=(ends, ends),
        in_specs=[HBM],
        out_specs=(VMEM, VMEM),
        scratch_shapes=[pltpu.SemaphoreType.DMA((2, HIGH))],
        compiler_params=params(2),
        name="ends",
    )(placed_in(fields[0], pltpu.HBM))
    lon_first = swap(lon_first, "lon", FIRST["lon"])
    lon_second = swap(lon_second, "lon", 1 - FIRST["lon"])
    small = (
        offsets[0].transpose(0, 2, 1),
        send_owner[0, 0],
        send_cell[0, 0],
        send_target[0, 0],
        send_frac[0, 0, 0],
    )
    large = (fractions[0], fields.reshape(channels * row_count, lanes))
    part = f32(groups, channels, lanes)
    rows, first, last, ninth, weights, *small = pl.pallas_call(
        own_kernel,
        out_shape=(
            f32(row_count, channels, lanes),
            part,
            part,
            part,
            f32(8, row_count, lanes),
            *(pltpu.SMEM(given.shape, given.dtype) for given in (send_count[0], *small)),
        ),
        in_specs=[SMEM] + [HBM] * 7,
        out_specs=(VMEM,) * 5 + (SMEM,) * 6,
        scratch_shapes=[pltpu.VMEM(given.shape, given.dtype) for given in large]
        + [pltpu.SemaphoreType.DMA((7,))],
        cost_estimate=pl.CostEstimate(flops=400000, bytes_accessed=800000, transcendentals=0),
        compiler_params=params(4),
        name="own",
    )(send_count[0], *(placed_in(given, pltpu.HBM) for given in large + small))
    small = [placed_in(given, pltpu.SMEM) for given in small]
    strips = f32(groups + 1, channels, lanes)
    lat_first, lat_second = pl.pallas_call(
        sides_kernel,
        out_shape=(strips, strips),
        in_specs=[VMEM] * 5,
        out_specs=(VMEM, VMEM),
        compiler_params=params(2),
        name="sides",
    )(lon_first, lon_second, first, last, ninth)
    lat_first = swap(lat_first, "lat", FIRST["lat"])
    lat_second = swap(lat_second, "lat", 1 - FIRST["lat"])
    centers = pl.pallas_call(
        center_kernel,
        out_shape=f32(tiles, 4, WINDOW, channels, lanes),
        in_specs=[SMEM] + [VMEM] * 3,
        out_specs=VMEM,
        scratch_shapes=[pltpu.VMEM((ext, channels, lanes), jnp.float32)],
        cost_estimate=pl.CostEstimate(flops=400000, bytes_accessed=3000000, transcendentals=0),
        compiler_params=params(4),
        name="centers",
    )(small[1], rows, lon_first, lon_second)
    columns, message = pl.pallas_call(
        advect_kernel,
        out_shape=(
            pltpu.VMEM((channels * row_count, lanes), jnp.float32),
            f32(2 * lon_count * width // lanes, lanes),
        ),
        in_specs=[SMEM] * 6 + [VMEM] * 4,
        out_specs=(VMEM, VMEM),
        scratch_shapes=[
            pltpu.VMEM((row_count, channels, lanes), jnp.float32),
            pltpu.VMEM((groups + 1, channels, lanes), jnp.float32),
            pltpu.VMEM((groups + 1, channels, lanes), jnp.float32),
            pltpu.VMEM((groups + 1, channels, lanes), jnp.float32),
        ],
        compiler_params=params(8),
        name="advect",
    )(*small, centers, weights, lat_first, lat_second)
    group = [0] * (2 * lon_count)
    for panel in range(2):
        for lon in range(lon_count):
            group[place_of(panel, lon, lon_count)] = panel * lon_count + lon
    received = lax.all_to_all(
        message.reshape(2 * lon_count, 1, width),
        ("panel", "lon"),
        0,
        0,
        tiled=True,
        axis_index_groups=[group],
    )
    out = pl.pallas_call(
        functools.partial(finish_kernel, lon_count),
        out_shape=pltpu.HBM((channels, row_count, lanes), jnp.float32),
        in_specs=[VMEM, VMEM],
        out_specs=HBM,
        scratch_shapes=[
            pltpu.VMEM((channels, TILE, lanes), jnp.float32),
            pltpu.SemaphoreType.DMA((tiles,)),
        ],
        compiler_params=params(2),
        name="finish",
    )(received.reshape(message.shape), columns.reshape(channels, row_count, lanes))
    return out[None]


def solution(mesh):
    placed = (
        P("panel", None, "lon", "lat"),
        P("panel", None, "lon", "lat"),
        P("panel", None, "lon", "lat"),
        P("panel", "lon", "lat"),
        P("panel", "lon", "lat", None),
        P("panel", "lon", "lat", None),
        P("panel", "lon", "lat", None),
        P("panel", "lon", "lat", None, None),
    )
    return jax.shard_map(
        body, mesh=mesh, in_specs=placed, out_specs=P("panel", None, "lon", "lat"), check_vma=False
    )
```

```python
import functools

import jax
import jax.numpy as jnp
from jax import lax
from jax.experimental import pallas as pl
from jax.experimental.pallas import tpu as pltpu
from jax.sharding import PartitionSpec as P

TILE = 8
LOW = 8
HIGH = 9
WINDOW = TILE + 3
LANES = 128
PITCH = 8
GROUP = LANES // PITCH
FIRST = {"lon": 1, "lat": 0}
ROOT = (1, 20)
FIELD = 32

VMEM = pl.BlockSpec(memory_space=pltpu.VMEM)
ANY = pl.BlockSpec(memory_space=pl.ANY)
HBM = pl.BlockSpec(memory_space=pltpu.HBM)
SMEM = pl.BlockSpec(memory_space=pltpu.SMEM)


def lane_iota(shape):
    return lax.broadcasted_iota(jnp.int32, shape, len(shape) - 1)


def place_of(panel, lon, lon_count):
    return (panel ^ ROOT[0]) * lon_count + (lon + lon_count - ROOT[1] % lon_count) % lon_count


def placed_in(array, space):
    return pltpu.with_memory_space_constraint(array, space)


def up_first(axis):
    return lax.axis_index(axis) % 2 == FIRST[axis]


def params(mib):
    return pltpu.CompilerParams(vmem_limit_bytes=mib * 1024 * 1024)


def ends_kernel(cells_ref, first_step_ref, second_step_ref, sems):
    row_count = cells_ref.shape[1]
    up = up_first("lon")
    copies = []
    for step, out_ref in enumerate((first_step_ref, second_step_ref)):
        upward = up if step == 0 else jnp.logical_not(up)
        for i in range(HIGH):
            row = jnp.where(upward, min(row_count - LOW + i, row_count - 1), i)
            copies.append(
                pltpu.make_async_copy(cells_ref.at[:, row, :], out_ref.at[i], sems.at[step, i])
            )
            copies[-1].start()
    for copy in copies:
        copy.wait()


def pack(rows, first, last, ninth):
    lane = lane_iota(rows[0][1].shape)
    for e, row in rows:
        g, base = e // GROUP, PITCH * (e % GROUP)
        turned = pltpu.roll(row, base, 1) if base else row
        first[g] = jnp.where((lane >= base) & (lane < base + PITCH), turned, first[g])
        below = (base - PITCH) % LANES
        last[g] = jnp.where((lane >= below) & (lane < below + PITCH), turned, last[g])
        ninth[g] = jnp.where(lane == (base + PITCH) % LANES, turned, ninth[g])


def own_kernel(
    count_ref, fractions_in, cells_in, offsets_in, owner_in, cell_in, target_in, frac_in,
    rows_ref, first_ref, last_ref, ninth_ref, weights_ref,
    count_out, offsets_out, owner_out, cell_out, target_out, frac_out,
    fractions_ref, cells_ref, sems,
):
    moves = (
        (cells_in, cells_ref),
        (fractions_in, fractions_ref),
        (offsets_in, offsets_out),
        (owner_in, owner_out),
        (cell_in, cell_out),
        (target_in, target_out),
        (frac_in, frac_out),
    )
    copies = [pltpu.make_async_copy(*move, sems.at[n]) for n, move in enumerate(moves)]
    for copy in copies:
        copy.start()
    count_out[0, 0] = count_ref[0, 0]
    row_count, channels, lanes = rows_ref.shape
    copies[0].wait()
    rows = []
    for i in range(row_count):
        row = cells_ref[pl.ds(i, channels, stride=row_count), :]
        rows_ref[i] = row
        rows.append((i + LOW, row))
    empty = jnp.zeros((channels, lanes), jnp.float32)
    first, last, ninth = ([empty] * first_ref.shape[0] for _ in range(3))
    pack(rows, first, last, ninth)
    for g in range(first_ref.shape[0]):
        first_ref[g], last_ref[g], ninth_ref[g] = first[g], last[g], ninth[g]
    copies[1].wait()
    for axis in range(2):
        x = fractions_ref[axis]
        weights_ref[4 * axis] = -x * (x - 1.0) * (x - 2.0) / 6.0
        weights_ref[4 * axis + 1] = (x + 1.0) * (x - 1.0) * (x - 2.0) / 2.0
        weights_ref[4 * axis + 2] = -(x + 1.0) * x * (x - 2.0) / 2.0
        weights_ref[4 * axis + 3] = (x + 1.0) * x * (x - 1.0) / 6.0
    for copy in copies[2:]:
        copy.wait()


def sides_kernel(
    from_first_ref, from_second_ref, first_ref, last_ref, ninth_ref, first_step_ref, second_step_ref
):
    groups, channels, lanes = first_ref.shape
    up = up_first("lon")
    prev = [jnp.where(up, from_second_ref[i], from_first_ref[i]) for i in range(LOW)]
    next_ = [jnp.where(up, from_first_ref[i], from_second_ref[i]) for i in range(HIGH)]
    first, last, ninth = ([ref[g] for g in range(groups)] for ref in (first_ref, last_ref, ninth_ref))
    after = groups * GROUP - LOW
    pack([(i, prev[i]) for i in range(LOW)], first, last, ninth)
    pack([(after + i, next_[i]) for i in range(LOW)], first, last, ninth)
    lane = lane_iota((channels, lanes))
    within = lane & (PITCH - 1)
    mixed = ninth[0]
    for g in range(1, groups):
        mixed = jnp.where(within == g, pltpu.roll(ninth[g], g, 1), mixed)
    low_part, high_part = pltpu.roll(next_[LOW], 3, 1), pltpu.roll(next_[LOW], 6, 1)
    mixed = jnp.where((lane >= 3) & (lane < 8), low_part, mixed)
    mixed = jnp.where((lane >= 11) & (lane < 15), high_part, mixed)
    first.append(mixed)
    last.append(next_[LOW])
    up = up_first("lat")
    for g in range(groups + 1):
        first_step_ref[g] = jnp.where(up, last[g], first[g])
        second_step_ref[g] = jnp.where(up, first[g], last[g])


def shift_of(offsets_ref, t, b):
    return offsets_ref[1, 0, t] - 1 + b


def center_kernel(
    offsets_ref, rows_ref, from_first_ref, from_second_ref, centers_ref, ext_ref
):
    row_count, _, _ = rows_ref.shape
    up = up_first("lon")
    for i in range(LOW):
        ext_ref[i] = jnp.where(up, from_second_ref[i], from_first_ref[i])
    ext_ref[LOW : LOW + row_count] = rows_ref[...]
    for i in range(HIGH):
        ext_ref[LOW + row_count + i] = jnp.where(up, from_first_ref[i], from_second_ref[i])
    for t in range(row_count // TILE):
        start = t * TILE + LOW - 1 + offsets_ref[0, 0, t]
        for b in range(4):
            turn = (LANES - shift_of(offsets_ref, t, b)) & (LANES - 1)
            for j in range(WINDOW):
                centers_ref[t, b, j] = pltpu.roll(ext_ref[start + j], turn, 1)


def advect_kernel(
    count_ref, offsets_ref, owner_ref, cell_ref, target_ref, frac_ref, centers_ref, weights_ref, from_first_ref, from_second_ref,
    columns_ref, message_ref,
    advected_ref, east_ref, west_ref, ninth_ref, sums_ref, places_ref,
):
    row_count, channels, lanes = advected_ref.shape
    slots = owner_ref.shape[1]
    lane = lane_iota((channels, lanes))
    up = up_first("lat")
    groups = east_ref.shape[0] - 1
    for g in range(groups + 1):
        west_ref[g] = jnp.where(up, from_second_ref[g], from_first_ref[g])
    for g in range(groups):
        east_ref[g] = jnp.where(up, from_first_ref[g], from_second_ref[g])
    mixed = jnp.where(up, from_first_ref[groups], from_second_ref[groups])
    ninth_ref[0] = mixed
    for g in range(1, groups):
        ninth_ref[g] = pltpu.roll(mixed, LANES - g, 1)
    last_row = jnp.where(lane < 5, pltpu.roll(mixed, LANES - 3, 1), pltpu.roll(mixed, LANES - 6, 1))
    east_ref[groups] = last_row
    ninth_ref[groups] = last_row

    within = lane & (PITCH - 1)
    for t in range(row_count // TILE):
        offset_lat = offsets_ref[1, 0, t]
        start = t * TILE + LOW - 1 + offsets_ref[0, 0, t]
        from_east = within < offset_lat + 2
        weights, sums = {}, {}
        for j in range(WINDOW):
            e = start + j
            g, base = e >> 4, PITCH * (e & (GROUP - 1))
            packed = jnp.where(from_east, east_ref[g], west_ref[g])
            beyond = jnp.where(offset_lat + 2 == HIGH, (base + PITCH) & (LANES - 1), -1)
            shifted = []
            for b in range(4):
                shift = shift_of(offsets_ref, t, b)
                inside = (lane >= -shift) & (lane < LANES - shift)
                if b == 3:
                    packed = jnp.where(lane == beyond, ninth_ref[g], packed)
                halo = pltpu.roll(packed, (2 * LANES - base - shift) & (LANES - 1), 1)
                shifted.append(jnp.where(inside, centers_ref[t, b, j], halo))
            for i in range(max(j - 3, 0), min(j, TILE - 1) + 1):
                row, a = t * TILE + i, j - i
                if a == 0:
                    weights[i] = [weights_ref[4 + b, row : row + 1, :] for b in range(4)]
                inner = weights[i][0] * shifted[0]
                for b in range(1, 4):
                    inner = inner + weights[i][b] * shifted[b]
                part = weights_ref[a, row : row + 1, :] * inner
                sums[i] = part if a == 0 else sums[i] + part
                if a == 3:
                    advected_ref[row] = sums[i]
                    columns_ref[pl.ds(row, channels, stride=row_count), :] = sums[i]

    channel = lax.broadcasted_iota(jnp.int32, (channels, lanes), 0)
    one_lane = lane_iota((1, lanes))
    capacity = slots // 2
    halves = capacity * FIELD // lanes
    per_row = lanes // FIELD
    sums_ref[...] = jnp.zeros_like(sums_ref)
    empty = jnp.where((one_lane & (FIELD - 1)) == channels, jnp.float32(lanes), jnp.float32(0.0))
    for h in range(2 * halves + 1):
        places_ref[h] = empty
    taken = [jnp.int32(0), jnp.int32(0)]
    at_value = lane - channel
    for k in range(slots):
        cell = cell_ref[0, k]
        r, c = cell >> 7, cell & (lanes - 1)
        a, b = frac_ref[0, k], frac_ref[1, k]
        near = jnp.where(one_lane == c, 1.0 - b, jnp.where(one_lane == c + 1, b, 0.0))
        value = jnp.sum(
            advected_ref[r] * ((1.0 - a) * near) + advected_ref[r + 1] * (a * near),
            axis=1,
            keepdims=True,
        )
        live = k < count_ref[0, 0]
        side = (owner_ref[0, k] != 0).astype(jnp.int32)
        target = target_ref[0, k].astype(jnp.float32)
        position = jnp.where(side == 0, taken[0], taken[1])
        taken[0] = taken[0] + jnp.where(live & (side == 0), 1, 0)
        taken[1] = taken[1] + jnp.where(live & (side == 1), 1, 0)
        base = (position & (per_row - 1)) * FIELD
        half = position >> (per_row.bit_length() - 1)
        here = jnp.where(live, side * halves + half, 2 * halves)
        sums_ref[here] = jnp.where(at_value == base, value, sums_ref[here])
        places_ref[here] = jnp.where(one_lane == base + channels, target, places_ref[here])
    lon_count = message_ref.shape[0] // (2 * halves)
    other = 1 - lax.axis_index("panel")
    message_ref[...] = jnp.zeros_like(message_ref)
    for side in range(2):
        for h in range(halves):
            n = side * halves + h
            row = place_of(other, side * (lon_count - 1), lon_count) * halves + h
            message_ref[pl.ds(row, 1), :] = (
                jnp.sum(sums_ref[n], axis=0, keepdims=True) + places_ref[n]
            )


def finish_kernel(lon_count, received_ref, columns_ref, out_ref, held_ref, sems):
    channels, row_count, lanes = out_ref.shape
    tiles = row_count // TILE
    lon = lax.axis_index("lon")

    def tile_of(ref, t):
        return ref.at[:, pl.ds(pl.multiple_of(t * TILE, TILE), TILE), :]

    changed = jnp.where(lon == 0, 0, tiles - 1)
    copies = []
    for n in range(tiles - 1):
        t = n + jnp.where(lon == 0, 1, 0)
        copies.append(
            pltpu.make_async_copy(tile_of(columns_ref, t), tile_of(out_ref, t), sems.at[n])
        )
        copies[n].start()
    held_ref[...] = columns_ref[:, pl.ds(pl.multiple_of(changed * TILE, TILE), TILE), :]

    @pl.when((lon == 0) | (lon == lon_count - 1))
    def _():
        entries = received_ref.shape[0] // 2
        other = (1 - lax.axis_index("panel")) ^ ROOT[0]
        values = received_ref[pl.ds(other * entries, entries), :]
        lane = lane_iota((entries, lanes))
        chosen = []
        for q in range(lanes // FIELD):
            at = q * FIELD + channels
            place = values[:, at : at + 1].astype(jnp.int32)
            chosen.append(jnp.where(lane == place, 1.0, 0.0))
        spread = lax.dot_general(
            values,
            jnp.concatenate(chosen, axis=1),
            (((0,), (0,)), ((), ())),
            precision=lax.Precision.HIGHEST,
            preferred_element_type=jnp.float32,
        )
        rim = spread[0:channels, 0:lanes]
        for q in range(1, lanes // FIELD):
            rim = rim + spread[q * FIELD : q * FIELD + channels, q * lanes : (q + 1) * lanes]
        row = jnp.where(lon == 0, 0, TILE - 1)
        held_ref[:, pl.ds(row, 1), :] = rim.reshape(channels, 1, lanes)

    copies.append(pltpu.make_async_copy(held_ref, tile_of(out_ref, changed), sems.at[tiles - 1]))
    copies[tiles - 1].start()
    for copy in copies:
        copy.wait()


def f32(*shape):
    return jax.ShapeDtypeStruct(shape, jnp.float32)


def swap(array, axis, first):
    pairs = []
    for i in range(first, lax.axis_size(axis) - 1, 2):
        pairs += [(i, i + 1), (i + 1, i)]
    return lax.ppermute(array, axis, pairs)


def body(fields, offsets, fractions, send_count, send_owner, send_cell, send_target, send_frac):
    _, channels, row_count, lanes = fields.shape
    groups = (LOW + row_count + LOW) // GROUP
    tiles = row_count // TILE
    lon_count = lax.axis_size("lon")
    slots = send_owner.shape[-1]
    width = slots // 2 * FIELD
    ext = LOW + row_count + HIGH

    ends = f32(HIGH, channels, lanes)
    lon_first, lon_second = pl.pallas_call(
        ends_kernel,
        out_shape=(ends, ends),
        in_specs=[HBM],
        out_specs=(VMEM, VMEM),
        scratch_shapes=[pltpu.SemaphoreType.DMA((2, HIGH))],
        compiler_params=params(2),
        name="ends",
    )(placed_in(fields[0], pltpu.HBM))
    lon_first = swap(lon_first, "lon", FIRST["lon"])
    lon_second = swap(lon_second, "lon", 1 - FIRST["lon"])
    small = (
        offsets[0].transpose(0, 2, 1),
        send_owner[0, 0],
        send_cell[0, 0],
        send_target[0, 0],
        send_frac[0, 0, 0],
    )
    large = (fractions[0], fields.reshape(channels * row_count, lanes))
    part = f32(groups, channels, lanes)
    rows, first, last, ninth, weights, *small = pl.pallas_call(
        own_kernel,
        out_shape=(
            f32(row_count, channels, lanes),
            part,
            part,
            part,
            f32(8, row_count, lanes),
            *(pltpu.SMEM(given.shape, given.dtype) for given in (send_count[0], *small)),
        ),
        in_specs=[SMEM] + [HBM] * 7,
        out_specs=(VMEM,) * 5 + (SMEM,) * 6,
        scratch_shapes=[pltpu.VMEM(given.shape, given.dtype) for given in large]
        + [pltpu.SemaphoreType.DMA((7,))],
        cost_estimate=pl.CostEstimate(flops=400000, bytes_accessed=800000, transcendentals=0),
        compiler_params=params(4),
        name="own",
    )(send_count[0], *(placed_in(given, pltpu.HBM) for given in large + small))
    small = [placed_in(given, pltpu.SMEM) for given in small]
    strips = f32(groups + 1, channels, lanes)
    lat_first, lat_second = pl.pallas_call(
        sides_kernel,
        out_shape=(strips, strips),
        in_specs=[VMEM] * 5,
        out_specs=(VMEM, VMEM),
        compiler_params=params(2),
        name="sides",
    )(lon_first, lon_second, first, last, ninth)
    lat_first = swap(lat_first, "lat", FIRST["lat"])
    lat_second = swap(lat_second, "lat", 1 - FIRST["lat"])
    centers = pl.pallas_call(
        center_kernel,
        out_shape=f32(tiles, 4, WINDOW, channels, lanes),
        in_specs=[SMEM] + [VMEM] * 3,
        out_specs=VMEM,
        scratch_shapes=[pltpu.VMEM((ext, channels, lanes), jnp.float32)],
        cost_estimate=pl.CostEstimate(flops=400000, bytes_accessed=3000000, transcendentals=0),
        compiler_params=params(4),
        name="centers",
    )(small[1], rows, lon_first, lon_second)
    columns, message = pl.pallas_call(
        advect_kernel,
        out_shape=(
            pltpu.VMEM((channels * row_count, lanes), jnp.float32),
            f32(2 * lon_count * width // lanes, lanes),
        ),
        in_specs=[SMEM] * 6 + [VMEM] * 4,
        out_specs=(VMEM, VMEM),
        scratch_shapes=[
            pltpu.VMEM((row_count, channels, lanes), jnp.float32),
            pltpu.VMEM((groups + 1, channels, lanes), jnp.float32),
            pltpu.VMEM((groups + 1, channels, lanes), jnp.float32),
            pltpu.VMEM((groups + 1, channels, lanes), jnp.float32),
            pltpu.VMEM((2 * (width // lanes) + 1, channels, lanes), jnp.float32),
            pltpu.VMEM((2 * (width // lanes) + 1, 1, lanes), jnp.float32),
        ],
        compiler_params=params(8),
        name="advect",
    )(*small, centers, weights, lat_first, lat_second)
    group = [0] * (2 * lon_count)
    for panel in range(2):
        for lon in range(lon_count):
            group[place_of(panel, lon, lon_count)] = panel * lon_count + lon
    received = lax.all_to_all(
        message.reshape(2 * lon_count, 1, width),
        ("panel", "lon"),
        0,
        0,
        tiled=True,
        axis_index_groups=[group],
    )
    out = pl.pallas_call(
        functools.partial(finish_kernel, lon_count),
        out_shape=pltpu.HBM((channels, row_count, lanes), jnp.float32),
        in_specs=[VMEM, VMEM],
        out_specs=HBM,
        scratch_shapes=[
            pltpu.VMEM((channels, TILE, lanes), jnp.float32),
            pltpu.SemaphoreType.DMA((tiles,)),
        ],
        compiler_params=params(2),
        name="finish",
    )(received.reshape(message.shape), columns.reshape(channels, row_count, lanes))
    return out[None]


def solution(mesh):
    placed = (
        P("panel", None, "lon", "lat"),
        P("panel", None, "lon", "lat"),
        P("panel", None, "lon", "lat"),
        P("panel", "lon", "lat"),
        P("panel", "lon", "lat", None),
        P("panel", "lon", "lat", None),
        P("panel", "lon", "lat", None),
        P("panel", "lon", "lat", None, None),
    )
    return jax.shard_map(
        body, mesh=mesh, in_specs=placed, out_specs=P("panel", None, "lon", "lat"), check_vma=False
    )
```

```python
import functools

import jax
import jax.numpy as jnp
from jax import lax
from jax.experimental import pallas as pl
from jax.experimental.pallas import tpu as pltpu
from jax.sharding import PartitionSpec as P

TILE = 8
LOW = 8
HIGH = 9
WINDOW = TILE + 3
LANES = 128
PITCH = 8
GROUP = LANES // PITCH
FIRST = {"lon": 1, "lat": 0}
ROOT = (1, 20)
FIELD = 32

VMEM = pl.BlockSpec(memory_space=pltpu.VMEM)
ANY = pl.BlockSpec(memory_space=pl.ANY)
HBM = pl.BlockSpec(memory_space=pltpu.HBM)
SMEM = pl.BlockSpec(memory_space=pltpu.SMEM)


def lane_iota(shape):
    return lax.broadcasted_iota(jnp.int32, shape, len(shape) - 1)


def place_of(panel, lon, lon_count):
    return (panel ^ ROOT[0]) * lon_count + (lon + lon_count - ROOT[1] % lon_count) % lon_count


def placed_in(array, space):
    return pltpu.with_memory_space_constraint(array, space)


def up_first(axis):
    return lax.axis_index(axis) % 2 == FIRST[axis]


def params(mib):
    return pltpu.CompilerParams(vmem_limit_bytes=mib * 1024 * 1024)


def ends_kernel(cells_ref, first_step_ref, second_step_ref, sems):
    row_count = cells_ref.shape[1]
    up = up_first("lon")
    copies = []
    for step, out_ref in enumerate((first_step_ref, second_step_ref)):
        upward = up if step == 0 else jnp.logical_not(up)
        for i in range(HIGH):
            row = jnp.where(upward, min(row_count - LOW + i, row_count - 1), i)
            copies.append(
                pltpu.make_async_copy(cells_ref.at[:, row, :], out_ref.at[i], sems.at[step, i])
            )
            copies[-1].start()
    for copy in copies:
        copy.wait()


def pack(rows, first, last, ninth):
    lane = lane_iota(rows[0][1].shape)
    for e, row in rows:
        g, base = e // GROUP, PITCH * (e % GROUP)
        turned = pltpu.roll(row, base, 1) if base else row
        first[g] = jnp.where((lane >= base) & (lane < base + PITCH), turned, first[g])
        below = (base - PITCH) % LANES
        last[g] = jnp.where((lane >= below) & (lane < below + PITCH), turned, last[g])
        ninth[g] = jnp.where(lane == (base + PITCH) % LANES, turned, ninth[g])


def own_kernel(
    count_ref, fractions_in, cells_in, offsets_in, owner_in, cell_in, target_in, frac_in,
    rows_ref, first_ref, last_ref, ninth_ref, weights_ref,
    count_out, offsets_out, owner_out, cell_out, target_out, frac_out,
    fractions_ref, cells_ref, sems,
):
    moves = (
        (cells_in, cells_ref),
        (fractions_in, fractions_ref),
        (offsets_in, offsets_out),
        (owner_in, owner_out),
        (cell_in, cell_out),
        (target_in, target_out),
        (frac_in, frac_out),
    )
    copies = [pltpu.make_async_copy(*move, sems.at[n]) for n, move in enumerate(moves)]
    for copy in copies:
        copy.start()
    count_out[0, 0] = count_ref[0, 0]
    row_count, channels, lanes = rows_ref.shape
    copies[0].wait()
    rows = []
    for i in range(row_count):
        row = cells_ref[pl.ds(i, channels, stride=row_count), :]
        rows_ref[i] = row
        rows.append((i + LOW, row))
    empty = jnp.zeros((channels, lanes), jnp.float32)
    first, last, ninth = ([empty] * first_ref.shape[0] for _ in range(3))
    pack(rows, first, last, ninth)
    for g in range(first_ref.shape[0]):
        first_ref[g], last_ref[g], ninth_ref[g] = first[g], last[g], ninth[g]
    copies[1].wait()
    for axis in range(2):
        x = fractions_ref[axis]
        weights_ref[4 * axis] = -x * (x - 1.0) * (x - 2.0) / 6.0
        weights_ref[4 * axis + 1] = (x + 1.0) * (x - 1.0) * (x - 2.0) / 2.0
        weights_ref[4 * axis + 2] = -(x + 1.0) * x * (x - 2.0) / 2.0
        weights_ref[4 * axis + 3] = (x + 1.0) * x * (x - 1.0) / 6.0
    for copy in copies[2:]:
        copy.wait()


def sides_kernel(
    from_first_ref, from_second_ref, first_ref, last_ref, ninth_ref, first_step_ref, second_step_ref
):
    groups, channels, lanes = first_ref.shape
    up = up_first("lon")
    prev = [jnp.where(up, from_second_ref[i], from_first_ref[i]) for i in range(LOW)]
    next_ = [jnp.where(up, from_first_ref[i], from_second_ref[i]) for i in range(HIGH)]
    first, last, ninth = ([ref[g] for g in range(groups)] for ref in (first_ref, last_ref, ninth_ref))
    after = groups * GROUP - LOW
    pack([(i, prev[i]) for i in range(LOW)], first, last, ninth)
    pack([(after + i, next_[i]) for i in range(LOW)], first, last, ninth)
    lane = lane_iota((channels, lanes))
    within = lane & (PITCH - 1)
    mixed = ninth[0]
    for g in range(1, groups):
        mixed = jnp.where(within == g, pltpu.roll(ninth[g], g, 1), mixed)
    low_part, high_part = pltpu.roll(next_[LOW], 3, 1), pltpu.roll(next_[LOW], 6, 1)
    mixed = jnp.where((lane >= 3) & (lane < 8), low_part, mixed)
    mixed = jnp.where((lane >= 11) & (lane < 15), high_part, mixed)
    first.append(mixed)
    last.append(next_[LOW])
    up = up_first("lat")
    for g in range(groups + 1):
        first_step_ref[g] = jnp.where(up, last[g], first[g])
        second_step_ref[g] = jnp.where(up, first[g], last[g])


def shift_of(offsets_ref, t, b):
    return offsets_ref[1, 0, t] - 1 + b


def center_kernel(
    offsets_ref, rows_ref, from_first_ref, from_second_ref, centers_ref, ext_ref
):
    row_count, _, _ = rows_ref.shape
    up = up_first("lon")
    for i in range(LOW):
        ext_ref[i] = jnp.where(up, from_second_ref[i], from_first_ref[i])
    ext_ref[LOW : LOW + row_count] = rows_ref[...]
    for i in range(HIGH):
        ext_ref[LOW + row_count + i] = jnp.where(up, from_first_ref[i], from_second_ref[i])
    for t in range(row_count // TILE):
        start = t * TILE + LOW - 1 + offsets_ref[0, 0, t]
        for b in range(4):
            turn = (LANES - shift_of(offsets_ref, t, b)) & (LANES - 1)
            for j in range(WINDOW):
                centers_ref[t, b, j] = pltpu.roll(ext_ref[start + j], turn, 1)


def advect_kernel(
    count_ref, offsets_ref, owner_ref, cell_ref, target_ref, frac_ref, centers_ref, weights_ref, from_first_ref, from_second_ref,
    columns_ref, message_ref,
    advected_ref, east_ref, west_ref, ninth_ref,
):
    row_count, channels, lanes = advected_ref.shape
    slots = owner_ref.shape[1]
    lane = lane_iota((channels, lanes))
    up = up_first("lat")
    groups = east_ref.shape[0] - 1
    for g in range(groups + 1):
        west_ref[g] = jnp.where(up, from_second_ref[g], from_first_ref[g])
    for g in range(groups):
        east_ref[g] = jnp.where(up, from_first_ref[g], from_second_ref[g])
    mixed = jnp.where(up, from_first_ref[groups], from_second_ref[groups])
    ninth_ref[0] = mixed
    for g in range(1, groups):
        ninth_ref[g] = pltpu.roll(mixed, LANES - g, 1)
    last_row = jnp.where(lane < 5, pltpu.roll(mixed, LANES - 3, 1), pltpu.roll(mixed, LANES - 6, 1))
    east_ref[groups] = last_row
    ninth_ref[groups] = last_row

    within = lane & (PITCH - 1)
    for t in range(row_count // TILE):
        offset_lat = offsets_ref[1, 0, t]
        start = t * TILE + LOW - 1 + offsets_ref[0, 0, t]
        from_east = within < offset_lat + 2
        weights, sums = {}, {}
        for j in range(WINDOW):
            e = start + j
            g, base = e >> 4, PITCH * (e & (GROUP - 1))
            packed = jnp.where(from_east, east_ref[g], west_ref[g])
            beyond = jnp.where(offset_lat + 2 == HIGH, (base + PITCH) & (LANES - 1), -1)
            shifted = []
            for b in range(4):
                shift = shift_of(offsets_ref, t, b)
                inside = (lane >= -shift) & (lane < LANES - shift)
                if b == 3:
                    packed = jnp.where(lane == beyond, ninth_ref[g], packed)
                halo = pltpu.roll(packed, (2 * LANES - base - shift) & (LANES - 1), 1)
                shifted.append(jnp.where(inside, centers_ref[t, b, j], halo))
            for i in range(max(j - 3, 0), min(j, TILE - 1) + 1):
                row, a = t * TILE + i, j - i
                if a == 0:
                    weights[i] = [weights_ref[4 + b, row : row + 1, :] for b in range(4)]
                inner = weights[i][0] * shifted[0]
                for b in range(1, 4):
                    inner = inner + weights[i][b] * shifted[b]
                part = weights_ref[a, row : row + 1, :] * inner
                sums[i] = part if a == 0 else sums[i] + part
                if a == 3:
                    advected_ref[row] = sums[i]
                    columns_ref[pl.ds(row, channels, stride=row_count), :] = sums[i]

    channel = lax.broadcasted_iota(jnp.int32, (channels, lanes), 0)
    one_lane = lane_iota((1, lanes))
    capacity = slots // 2
    halves = capacity * FIELD // lanes
    per_row = lanes // FIELD
    sums = [jnp.zeros((channels, lanes), jnp.float32) for _ in range(2 * halves)]
    empty = jnp.where((one_lane & (FIELD - 1)) == channels, jnp.float32(lanes), jnp.float32(0.0))
    places = [empty for _ in range(2 * halves)]
    taken = [jnp.int32(0), jnp.int32(0)]
    at_value = lane - channel
    for k in range(slots):
        cell = cell_ref[0, k]
        r, c = cell >> 7, cell & (lanes - 1)
        a, b = frac_ref[0, k], frac_ref[1, k]
        near = jnp.where(one_lane == c, 1.0 - b, jnp.where(one_lane == c + 1, b, 0.0))
        value = jnp.sum(
            advected_ref[r] * ((1.0 - a) * near) + advected_ref[r + 1] * (a * near),
            axis=1,
            keepdims=True,
        )
        live = k < count_ref[0, 0]
        side = (owner_ref[0, k] != 0).astype(jnp.int32)
        target = target_ref[0, k].astype(jnp.float32)
        position = jnp.where(side == 0, taken[0], taken[1])
        taken[0] = taken[0] + jnp.where(live & (side == 0), 1, 0)
        taken[1] = taken[1] + jnp.where(live & (side == 1), 1, 0)
        base = (position % per_row) * FIELD
        here = jnp.where(live, side * halves + position // per_row, -1)
        for h in range(2 * halves):
            lane_base = jnp.where(here == h, base, -lanes)
            sums[h] = jnp.where(at_value == lane_base, value, sums[h])
            places[h] = jnp.where(one_lane == lane_base + channels, target, places[h])
    lon_count = message_ref.shape[0] // (2 * halves)
    other = 1 - lax.axis_index("panel")
    message_ref[...] = jnp.zeros_like(message_ref)
    for side in range(2):
        for h in range(halves):
            n = side * halves + h
            row = place_of(other, side * (lon_count - 1), lon_count) * halves + h
            message_ref[pl.ds(row, 1), :] = jnp.sum(sums[n], axis=0, keepdims=True) + places[n]


def finish_kernel(lon_count, received_ref, columns_ref, out_ref, held_ref, sems):
    channels, row_count, lanes = out_ref.shape
    tiles = row_count // TILE
    lon = lax.axis_index("lon")
    lowest = lon == 0

    def copy_rows(n, first, count):
        rows = (slice(None), pl.ds(first, count), slice(None))
        return pltpu.make_async_copy(columns_ref.at[rows], out_ref.at[rows], sems.at[n])

    copies = []
    for n in range(tiles - 1):
        first = (n + jnp.where(lowest, 1, 0)) * TILE
        copies.append(copy_rows(n, pl.multiple_of(first, TILE), TILE))
    copies.append(copy_rows(tiles - 1, jnp.where(lowest, 1, row_count - TILE), TILE - 1))
    for copy in copies:
        copy.start()
    changed = jnp.where(lowest, 0, row_count - 1)
    held_ref[...] = columns_ref[:, pl.ds(changed, 1), :]

    @pl.when((lon == 0) | (lon == lon_count - 1))
    def _():
        entries = received_ref.shape[0] // 2
        other = (1 - lax.axis_index("panel")) ^ ROOT[0]
        values = received_ref[pl.ds(other * entries, entries), :]
        lane = lane_iota((entries, lanes))
        chosen = []
        for q in range(lanes // FIELD):
            at = q * FIELD + channels
            place = values[:, at : at + 1].astype(jnp.int32)
            chosen.append(jnp.where(lane == place, 1.0, 0.0))
        spread = lax.dot_general(
            values,
            jnp.concatenate(chosen, axis=1),
            (((0,), (0,)), ((), ())),
            precision=lax.Precision.HIGHEST,
            preferred_element_type=jnp.float32,
        )
        rim = spread[0:channels, 0:lanes]
        for q in range(1, lanes // FIELD):
            rim = rim + spread[q * FIELD : q * FIELD + channels, q * lanes : (q + 1) * lanes]
        held_ref[...] = rim.reshape(channels, 1, lanes)

    target = out_ref.at[:, pl.ds(changed, 1), :]
    copies.append(pltpu.make_async_copy(held_ref, target, sems.at[tiles]))
    copies[tiles].start()
    for copy in copies:
        copy.wait()


def f32(*shape):
    return jax.ShapeDtypeStruct(shape, jnp.float32)


def swap(array, axis, first):
    pairs = []
    for i in range(first, lax.axis_size(axis) - 1, 2):
        pairs += [(i, i + 1), (i + 1, i)]
    return lax.ppermute(array, axis, pairs)


def body(fields, offsets, fractions, send_count, send_owner, send_cell, send_target, send_frac):
    _, channels, row_count, lanes = fields.shape
    groups = (LOW + row_count + LOW) // GROUP
    tiles = row_count // TILE
    lon_count = lax.axis_size("lon")
    slots = send_owner.shape[-1]
    width = slots // 2 * FIELD
    ext = LOW + row_count + HIGH

    ends = f32(HIGH, channels, lanes)
    lon_first, lon_second = pl.pallas_call(
        ends_kernel,
        out_shape=(ends, ends),
        in_specs=[HBM],
        out_specs=(VMEM, VMEM),
        scratch_shapes=[pltpu.SemaphoreType.DMA((2, HIGH))],
        compiler_params=params(2),
        name="ends",
    )(placed_in(fields[0], pltpu.HBM))
    lon_first = swap(lon_first, "lon", FIRST["lon"])
    lon_second = swap(lon_second, "lon", 1 - FIRST["lon"])
    small = (
        offsets[0].transpose(0, 2, 1),
        send_owner[0, 0],
        send_cell[0, 0],
        send_target[0, 0],
        send_frac[0, 0, 0],
    )
    large = (fractions[0], fields.reshape(channels * row_count, lanes))
    part = f32(groups, channels, lanes)
    rows, first, last, ninth, weights, *small = pl.pallas_call(
        own_kernel,
        out_shape=(
            f32(row_count, channels, lanes),
            part,
            part,
            part,
            f32(8, row_count, lanes),
            *(pltpu.SMEM(given.shape, given.dtype) for given in (send_count[0], *small)),
        ),
        in_specs=[SMEM] + [HBM] * 7,
        out_specs=(VMEM,) * 5 + (SMEM,) * 6,
        scratch_shapes=[pltpu.VMEM(given.shape, given.dtype) for given in large]
        + [pltpu.SemaphoreType.DMA((7,))],
        cost_estimate=pl.CostEstimate(flops=400000, bytes_accessed=800000, transcendentals=0),
        compiler_params=params(4),
        name="own",
    )(send_count[0], *(placed_in(given, pltpu.HBM) for given in large + small))
    small = [placed_in(given, pltpu.SMEM) for given in small]
    strips = f32(groups + 1, channels, lanes)
    lat_first, lat_second = pl.pallas_call(
        sides_kernel,
        out_shape=(strips, strips),
        in_specs=[VMEM] * 5,
        out_specs=(VMEM, VMEM),
        compiler_params=params(2),
        name="sides",
    )(lon_first, lon_second, first, last, ninth)
    lat_first = swap(lat_first, "lat", FIRST["lat"])
    lat_second = swap(lat_second, "lat", 1 - FIRST["lat"])
    centers = pl.pallas_call(
        center_kernel,
        out_shape=f32(tiles, 4, WINDOW, channels, lanes),
        in_specs=[SMEM] + [VMEM] * 3,
        out_specs=VMEM,
        scratch_shapes=[pltpu.VMEM((ext, channels, lanes), jnp.float32)],
        cost_estimate=pl.CostEstimate(flops=400000, bytes_accessed=3000000, transcendentals=0),
        compiler_params=params(4),
        name="centers",
    )(small[1], rows, lon_first, lon_second)
    columns, message = pl.pallas_call(
        advect_kernel,
        out_shape=(
            pltpu.VMEM((channels * row_count, lanes), jnp.float32),
            f32(2 * lon_count * width // lanes, lanes),
        ),
        in_specs=[SMEM] * 6 + [VMEM] * 4,
        out_specs=(VMEM, VMEM),
        scratch_shapes=[
            pltpu.VMEM((row_count, channels, lanes), jnp.float32),
            pltpu.VMEM((groups + 1, channels, lanes), jnp.float32),
            pltpu.VMEM((groups + 1, channels, lanes), jnp.float32),
            pltpu.VMEM((groups + 1, channels, lanes), jnp.float32),
        ],
        compiler_params=params(8),
        name="advect",
    )(*small, centers, weights, lat_first, lat_second)
    group = [0] * (2 * lon_count)
    for panel in range(2):
        for lon in range(lon_count):
            group[place_of(panel, lon, lon_count)] = panel * lon_count + lon
    received = lax.all_to_all(
        message.reshape(2 * lon_count, 1, width),
        ("panel", "lon"),
        0,
        0,
        tiled=True,
        axis_index_groups=[group],
    )
    out = pl.pallas_call(
        functools.partial(finish_kernel, lon_count),
        out_shape=pltpu.HBM((channels, row_count, lanes), jnp.float32),
        in_specs=[VMEM, VMEM],
        out_specs=HBM,
        scratch_shapes=[
            pltpu.VMEM((channels, 1, lanes), jnp.float32),
            pltpu.SemaphoreType.DMA((tiles + 1,)),
        ],
        compiler_params=params(2),
        name="finish",
    )(received.reshape(message.shape), columns.reshape(channels, row_count, lanes))
    return out[None]


def solution(mesh):
    placed = (
        P("panel", None, "lon", "lat"),
        P("panel", None, "lon", "lat"),
        P("panel", None, "lon", "lat"),
        P("panel", "lon", "lat"),
        P("panel", "lon", "lat", None),
        P("panel", "lon", "lat", None),
        P("panel", "lon", "lat", None),
        P("panel", "lon", "lat", None, None),
    )
    return jax.shard_map(
        body, mesh=mesh, in_specs=placed, out_specs=P("panel", None, "lon", "lat"), check_vma=False
    )
```
